256 devices in a mesh: tm: 8 (over z_hi, core), row: 2 (over z_lo), col: 16 (over y, x).
Axes of the slice: x: 4, y: 4, z: 8 (z_hi: 4, z_lo: 2; z = z_hi * 2 + z_lo), core: 2. Of those that a mesh axis runs over, the one named last changes fastest.
Arguments:
- latent: bfloat16 [16, 16, 128, 384], P('tm', 'row', 'col'), may hold values from -6 to 6
- grad_out: bfloat16 [16, 16, 128, 384], P('tm', 'row', 'col'), may hold values from -6 to 6
- norm_gain: float32 [384], replicated, may hold values from 0.1 to 1.9
- w_query: bfloat16 [384, 384], replicated, may hold values from -0.3125 to 0.3125
- w_key: bfloat16 [384, 384], replicated, may hold values from -0.3125 to 0.3125
- w_value: bfloat16 [384, 384], replicated, may hold values from -0.3125 to 0.3125
- w_out: bfloat16 [384, 384], replicated, may hold values from -2.5 to 2.5
- gain_one: float32 [384], replicated, may hold values from 0.1 to 1.9
- gain_two: float32 [384], replicated, may hold values from 0.1 to 1.9
- kernel_one: bfloat16 [3, 3, 3, 384, 384], P(None, None, None, 'col'), may hold values from -0.0625 to 0.0625
- kernel_two: bfloat16 [3, 3, 3, 384, 384], P(None, None, None, 'col'), may hold values from -0.0625 to 0.0625
Outputs:
- grad_in: float32 [16, 16, 128, 384], P('tm', 'row', 'col')
The draws below stay inside these ranges and needn't reach their ends.
All inputs are finite; a program needn't handle non-finite values.
Results may differ from the reference program's by a relative error of at most 0.017.
Values may be sent and summed in bfloat16 or wider, within the bound.
No kernel may reach another device: no remote copies, remote signals or barrier semaphores. Data moves between devices by JAX's collectives and lax.ppermute only.
A program may use at most 128 MiB of HBM per device.

```python
import math
import jax
import jax.numpy as jnp
from jax import lax

C = 384
FRAMES = 16
H = 16
W = 128


def steps_of(rng, extent, pieces, least, top_value):
    loudness, own = 1.0, jax.random.fold_in(rng, 6)
    for dim, blocks in pieces:
        steps = jnp.exp(jax.random.uniform(jax.random.fold_in(own, dim), (blocks,), jnp.float32, least / len(pieces), top_value / len(pieces)))
        loudness = loudness * jnp.repeat(steps, extent[dim] // blocks).reshape([-1 if axis == dim else 1 for axis in range(len(extent))])
    return loudness


def scatter_about(stream_key, shape, spread, limit, pieces=(), kind=jnp.bfloat16):
    result = spread * jax.random.normal(stream_key, shape, jnp.float32)
    if pieces:
        result = result * steps_of(stream_key, shape, pieces, -0.22, 0.18)
    return jnp.clip(result, -limit, limit).astype(kind)


def setup_inputs(seed: int = 0) -> dict:
    key_list = jax.random.split(jax.random.key(seed), 12)
    return {
        "latent": scatter_about(key_list[0], (FRAMES, H, W, C), 1.0, 6.0, ((0, 8), (1, 2), (2, 16))),
        "grad_out": scatter_about(key_list[1], (FRAMES, H, W, C), 1.0, 6.0, ((0, 8), (1, 2), (2, 16))),
        "norm_gain": jnp.clip(1.0 + 0.18 * jax.random.normal(key_list[2], (C,), jnp.float32), 0.1, 1.9),
        "w_query": scatter_about(key_list[3], (C, C), C ** -0.5, 0.3125),
        "w_key": scatter_about(key_list[4], (C, C), C ** -0.5, 0.3125),
        "w_value": scatter_about(key_list[5], (C, C), C ** -0.5, 0.3125),
        "w_out": scatter_about(key_list[6], (C, C), (max(C // 64, 1)) ** -0.5, 2.5),
        "gain_one": jnp.clip(1.0 + 0.18 * jax.random.normal(key_list[7], (C,), jnp.float32), 0.1, 1.9),
        "gain_two": jnp.clip(1.0 + 0.18 * jax.random.normal(key_list[8], (C,), jnp.float32), 0.1, 1.9),
        "kernel_one": scatter_about(key_list[9], (3, 3, 3, C, C), (27 * C) ** -0.5, 0.0625, ((3, 16),)),
        "kernel_two": scatter_about(key_list[10], (3, 3, 3, C, C), (27 * C) ** -0.5, 0.0625, ((3, 16),)),
    }


EPSILON = 1e-06

def norm_factor(field):
    return lax.rsqrt(lax.optimization_barrier(jnp.mean(field * field, axis=-1, keepdims=True)) + EPSILON)

def norm_backward(field, gain, upstream):
    factor = norm_factor(field)
    gained = gain * upstream
    return factor * gained - field * factor ** 3 * lax.optimization_barrier(jnp.mean(field * gained, axis=-1, keepdims=True))

def silu_slope(pre):
    sig = jax.nn.sigmoid(pre)
    return sig * (1.0 + pre * (1.0 - sig))

def conv_taps(padded, kernel, frame_count, row_count, column_count, flipped):
    total = jnp.zeros((frame_count * row_count * column_count, kernel.shape[4]), jnp.float32)
    for depth in range(3):
        for down in range(3):
            for across in range(3):
                if flipped:
                    start_t, start_r, start_c = (2 - depth, 2 - down, 2 - across)
                    matrix = kernel[depth, down, across].T
                else:
                    start_t, start_r, start_c = (depth, down, across)
                    matrix = kernel[depth, down, across]
                window = padded[start_t:start_t + frame_count, start_r:start_r + row_count, start_c:start_c + column_count]
                window = window.reshape(-1, padded.shape[3])
                total = total + jnp.dot(window, matrix, preferred_element_type=jnp.float32)
    return total.reshape(frame_count, row_count, column_count, -1)

def reference(latent, grad_out, norm_gain, w_query, w_key, w_value, w_out, gain_one, gain_two, kernel_one, kernel_two):
    frame_count, row_count, column_count, channels = latent.shape
    positions = row_count * column_count
    inverse_root = 1.0 / math.sqrt(channels)
    wide_latent = latent.astype(jnp.float32)
    normed = (wide_latent * norm_factor(wide_latent) * norm_gain).astype(jnp.bfloat16).reshape(-1, channels)
    queries = jnp.dot(normed, w_query, preferred_element_type=jnp.float32).astype(jnp.bfloat16).reshape(frame_count, positions, channels)
    keys = jnp.dot(normed, w_key, preferred_element_type=jnp.float32).astype(jnp.bfloat16).reshape(frame_count, positions, channels)
    values = jnp.dot(normed, w_value, preferred_element_type=jnp.float32).astype(jnp.bfloat16).reshape(frame_count, positions, channels)

    def frame_forward(operands):
        frame_q, frame_k, frame_v = operands
        prob = jax.nn.softmax(jnp.dot(frame_q, frame_k.T, preferred_element_type=jnp.float32) * inverse_root, axis=-1)
        return jnp.dot(prob.astype(jnp.bfloat16), frame_v, preferred_element_type=jnp.float32).astype(jnp.bfloat16)
    context = lax.map(frame_forward, (queries, keys, values))
    mixed = wide_latent + jnp.dot(context.reshape(-1, channels), w_out, preferred_element_type=jnp.float32).reshape(latent.shape)
    mixed = mixed.astype(jnp.bfloat16)
    wide_mixed = mixed.astype(jnp.float32)
    pre_one = wide_mixed * norm_factor(wide_mixed) * gain_one
    act_one = jax.nn.silu(pre_one).astype(jnp.bfloat16)
    padded = jnp.pad(act_one, ((2, 0), (1, 1), (1, 1), (0, 0)))
    conv_one = conv_taps(padded, kernel_one, frame_count, row_count, column_count, False).astype(jnp.bfloat16)
    wide_conv = conv_one.astype(jnp.float32)
    pre_two = wide_conv * norm_factor(wide_conv) * gain_two
    padded = jnp.pad(grad_out, ((0, 2), (1, 1), (1, 1), (0, 0)))
    g_act_two = conv_taps(padded, kernel_two, frame_count, row_count, column_count, True)
    g_conv = norm_backward(wide_conv, gain_two, g_act_two * silu_slope(pre_two)).astype(jnp.bfloat16)
    padded = jnp.pad(g_conv, ((0, 2), (1, 1), (1, 1), (0, 0)))
    g_act_one = conv_taps(padded, kernel_one, frame_count, row_count, column_count, True)
    g_mixed = grad_out.astype(jnp.float32) + norm_backward(wide_mixed, gain_one, g_act_one * silu_slope(pre_one))
    g_mixed = g_mixed.astype(jnp.bfloat16)
    g_context = jnp.dot(g_mixed.reshape(-1, channels), w_out.T, preferred_element_type=jnp.float32)
    g_context = g_context.astype(jnp.bfloat16).reshape(frame_count, positions, channels)

    def frame_backward(operands):
        frame_q, frame_k, frame_v, frame_g = operands
        prob = jax.nn.softmax(jnp.dot(frame_q, frame_k.T, preferred_element_type=jnp.float32) * inverse_root, axis=-1)
        prob_b = prob.astype(jnp.bfloat16)
        g_prob = jnp.dot(frame_g, frame_v.T, preferred_element_type=jnp.float32)
        g_score = (prob * (g_prob - lax.optimization_barrier(jnp.sum(prob * g_prob, axis=-1, keepdims=True))) * inverse_root).astype(jnp.bfloat16)
        g_query = jnp.dot(g_score, frame_k, preferred_element_type=jnp.float32)
        g_key = jnp.dot(g_score.T, frame_q, preferred_element_type=jnp.float32)
        g_value = jnp.dot(prob_b.T, frame_g, preferred_element_type=jnp.float32)
        return (g_query, g_key, g_value)
    g_query, g_key, g_value = lax.map(frame_backward, (queries, keys, values, g_context))
    highest = lax.Precision.HIGHEST
    g_normed = jnp.dot(g_query.reshape(-1, channels), w_query.astype(jnp.float32).T, precision=highest)
    g_normed = g_normed + jnp.dot(g_key.reshape(-1, channels), w_key.astype(jnp.float32).T, precision=highest)
    g_normed = g_normed + jnp.dot(g_value.reshape(-1, channels), w_value.astype(jnp.float32).T, precision=highest)
    g_normed = g_normed.reshape(latent.shape)
    return g_mixed.astype(jnp.float32) + norm_backward(wide_latent, norm_gain, g_normed)
```

```python
import math

import jax
import jax.numpy as jnp
from jax import lax
from jax.experimental import pallas as pl
from jax.experimental.pallas import tpu as pltpu
from jax.sharding import PartitionSpec as P

EPSILON = 1e-06
F32, BF16 = jnp.float32, jnp.bfloat16
C = 384
ROWS, SLOTS = 16, 16
SPAN = ROWS * SLOTS
VMEM = 50 * 1024 * 1024
NT = (((1,), (1,)), ((), ()))


def norm_factor(field):
    return lax.rsqrt(jnp.mean(field * field, axis=-1, keepdims=True) + EPSILON)


def norm_backward(field, gain, upstream):
    factor = norm_factor(field)
    gained = gain * upstream
    return factor * gained - field * factor**3 * jnp.mean(field * gained, axis=-1, keepdims=True)


def silu_slope(pre):
    sig = jax.nn.sigmoid(pre)
    return sig * (1.0 + pre * (1.0 - sig))


def stage_shifts(x_ref, s_ref):
    length = x_ref.shape[1]
    for frame in range(3):
        wide = x_ref[frame].astype(F32)
        s_ref[frame, :, :C] = pltpu.roll(wide, 1, 0).astype(BF16)
        s_ref[frame, :, C : 2 * C] = x_ref[frame]
        s_ref[frame, :, 2 * C :] = pltpu.roll(wide, length - 1, 0).astype(BF16)


def flipped_taps(s_ref, w_ref, step, pitch, span):
    depth, down = step // 3, lax.rem(step, 3)
    start = pl.multiple_of((2 - down) * pitch, pitch)
    total = None
    for across in range(3):
        lane = (2 - across) * C
        window = s_ref[2 - depth, pl.ds(start, span), lane : lane + C]
        term = lax.dot_general(window, w_ref[across], NT, preferred_element_type=F32)
        total = term if total is None else total + term
    return total


def pair_kernel(core_ref, x_ref, w_ref, out_ref, s_ref):
    step = pl.program_id(0)
    pitch, span = 2 * SLOTS, 2 * SPAN

    @pl.when(step == 0)
    def _():
        stage_shifts(x_ref, s_ref)
        out_ref[...] = jnp.zeros_like(out_ref)

    @pl.when(core_ref[0] == 0)
    def _():
        start = pl.multiple_of(lax.rem(step, 3) * pitch, pitch)
        window = s_ref[step // 3, pl.ds(start, span), :]
        out_ref[...] += jnp.dot(
            window, w_ref[...].reshape(3 * C, C), preferred_element_type=F32
        )

    @pl.when(core_ref[0] != 0)
    def _():
        out_ref[...] += flipped_taps(s_ref, w_ref, step, pitch, span)


def pair_conv(core, x, weights):
    return pl.pallas_call(
        pair_kernel,
        out_shape=jax.ShapeDtypeStruct((2 * SPAN, C), F32),
        grid_spec=pltpu.PrefetchScalarGridSpec(
            num_scalar_prefetch=1,
            grid=(9,),
            in_specs=[
                pl.BlockSpec(x.shape, lambda i, core: (0, 0, 0)),
                pl.BlockSpec((3, C, C), lambda i, core: (i, 0, 0)),
            ],
            out_specs=pl.BlockSpec((2 * SPAN, C), lambda i, core: (0, 0)),
            scratch_shapes=[pltpu.VMEM((3, x.shape[1], 3 * C), BF16)],
        ),
        compiler_params=pltpu.CompilerParams(vmem_limit_bytes=VMEM),
        cost_estimate=pl.CostEstimate(
            flops=2 * 27 * 2 * SPAN * C * C, bytes_accessed=27 * C * C * 2, transcendentals=0
        ),
        name="pair_conv",
    )(core, x, weights)


def own_slots(shape):
    slot = lax.rem(lax.broadcasted_iota(jnp.int32, shape, 0), SLOTS)
    return (slot >= 2) & (slot < 10)


def back_kernel(core_ref, x_ref, mine_ref, other_ref, grad_ref, mixed_ref, gain_ref, out_ref, s_ref, sum_ref):
    step = pl.program_id(0)

    @pl.when(step == 0)
    def _():
        stage_shifts(x_ref, s_ref)
        sum_ref[...] = jnp.zeros_like(sum_ref)

    @pl.when(core_ref[0] == 0)
    def _():
        sum_ref[...] += flipped_taps(s_ref, mine_ref, step, SLOTS, SPAN)

    @pl.when(core_ref[0] != 0)
    def _():
        sum_ref[...] += flipped_taps(s_ref, other_ref, step, SLOTS, SPAN)

    @pl.when(step == 8)
    def _():
        mixed = mixed_ref[...].astype(F32)
        gain = gain_ref[...]
        slope = silu_slope(mixed * norm_factor(mixed) * gain)
        total = grad_ref[...].astype(F32) + norm_backward(mixed, gain, sum_ref[...] * slope)
        out_ref[...] = jnp.where(own_slots(total.shape), total, 0.0).astype(BF16)


def back_conv(core, x, mine, other, grad, mixed, gain):
    whole = lambda i, core: (0, 0)
    return pl.pallas_call(
        back_kernel,
        out_shape=jax.ShapeDtypeStruct((SPAN, C), BF16),
        grid_spec=pltpu.PrefetchScalarGridSpec(
            num_scalar_prefetch=1,
            grid=(9,),
            in_specs=[
                pl.BlockSpec(x.shape, lambda i, core: (0, 0, 0)),
                pl.BlockSpec((3, C, C), lambda i, core: (i * (1 - core[0]), 0, 0)),
                pl.BlockSpec((3, C, C), lambda i, core: (i * core[0], 0, 0)),
                pl.BlockSpec((SPAN, C), whole),
                pl.BlockSpec((SPAN, C), whole),
                pl.BlockSpec((1, C), whole),
            ],
            out_specs=pl.BlockSpec((SPAN, C), whole),
            scratch_shapes=[pltpu.VMEM((3, x.shape[1], 3 * C), BF16), pltpu.VMEM((SPAN, C), F32)],
        ),
        compiler_params=pltpu.CompilerParams(vmem_limit_bytes=VMEM),
        cost_estimate=pl.CostEstimate(
            flops=2 * 27 * SPAN * C * C, bytes_accessed=27 * C * C * 2, transcendentals=0
        ),
        name="back_conv",
    )(core, x, mine, other, grad, mixed, gain)


CHUNK = 512


def attend_back_kernel(
    col_ref, gm_ref, prob_ref, keys_ref, values_ref, qk_ref, w_out_ref, w_value_ref, w_query_ref,
    out_ref, gp_ref, sum_ref, mix_ref, right_ref,
):
    positions = keys_ref.shape[0]
    count = positions // CHUNK
    inverse_root = 1.0 / math.sqrt(C)
    g_context = lax.dot_general(
        gm_ref[...], w_out_ref[...], NT, preferred_element_type=F32
    ).astype(BF16)
    right_ref[:SPAN, :] = qk_ref[...]
    right_ref[SPAN:, :] = lax.dot_general(
        g_context, w_value_ref[...], NT, preferred_element_type=F32
    ).astype(BF16)
    delta = jnp.zeros((1, SPAN), F32)
    for c in range(count):
        part = pl.ds(c * CHUNK, CHUNK)
        g_prob = lax.dot_general(values_ref[part, :], g_context, NT, preferred_element_type=F32)
        gp_ref[part, :] = g_prob
        delta = delta + jnp.sum(prob_ref[part, :] * g_prob, axis=0, keepdims=True)
    g_query = jnp.zeros((SPAN, C), F32)
    for c in range(count):
        part = pl.ds(c * CHUNK, CHUNK)
        prob = prob_ref[part, :]
        g_score = (prob * (gp_ref[part, :] - delta) * inverse_root).astype(BF16)
        mix_ref[:, :SPAN] = g_score
        mix_ref[:, SPAN:] = prob.astype(BF16)
        sum_ref[part, :] = jnp.dot(mix_ref[...], right_ref[...], preferred_element_type=F32)
        g_query += lax.dot_general(
            g_score, keys_ref[part, :], (((0,), (0,)), ((), ())), preferred_element_type=F32
        )
    high = g_query.astype(BF16)
    low = (g_query - high.astype(F32)).astype(BF16)
    local = lax.dot_general(high, w_query_ref[...], NT, preferred_element_type=F32)
    local += lax.dot_general(low, w_query_ref[...], NT, preferred_element_type=F32)
    local = pltpu.roll(local, SPAN - 2, 0)
    for r in range(ROWS):
        start = pl.multiple_of((r // 8) * (positions // 2) + col_ref[0] * 64 + (r % 8) * 8, 8)
        sum_ref[pl.ds(start, 8), :] += local[r * SLOTS : r * SLOTS + 8]
    out_ref[...] = sum_ref[...].astype(BF16)


def attend_back(col, gm, prob, keys, values, qk, w_out, w_value, w_query):
    positions = keys.shape[0]
    return pl.pallas_call(
        attend_back_kernel,
        out_shape=jax.ShapeDtypeStruct((positions, C), BF16),
        in_specs=[pl.BlockSpec(memory_space=pltpu.SMEM)] + [pl.BlockSpec(memory_space=pltpu.VMEM)] * 8,
        out_specs=pl.BlockSpec(memory_space=pltpu.VMEM),
        scratch_shapes=[
            pltpu.VMEM((positions, SPAN), F32),
            pltpu.VMEM((positions, C), F32),
            pltpu.VMEM((CHUNK, 2 * SPAN), BF16),
            pltpu.VMEM((2 * SPAN, C), BF16),
        ],
        compiler_params=pltpu.CompilerParams(vmem_limit_bytes=VMEM),
        name="attend_back",
    )(col, gm, prob, keys, values, qk, w_out, w_value, w_query)


def shards(
    latent,
    grad_out,
    norm_gain,
    w_query,
    w_key,
    w_value,
    w_out,
    gain_one,
    gain_two,
    kernel_one,
    kernel_two,
):
    time_row = ("tm", "row")
    tm, row, col = lax.axis_index("tm"), lax.axis_index("row"), lax.axis_index("col")
    groups, cols = lax.axis_size("tm"), lax.axis_size("col")
    frames = groups * 2
    core = lax.rem(tm, 2)
    core_arg, col_arg = core.reshape(1), col.reshape(1)
    inverse_root = 1.0 / math.sqrt(C)
    swap_core = [(i, i ^ 1) for i in range(groups)]
    swap_row = [(0, 1), (1, 0)]

    def moved(value, steps):
        pairs = [(s, s + steps) for s in range(frames) if 0 <= s + steps < frames]
        return lax.ppermute(value, time_row, pairs)

    mine = lax.all_gather(
        jnp.where(core == 0, kernel_one, kernel_two), "col", axis=3, tiled=True
    ).reshape(27, C, C)
    other = lax.ppermute(mine, "tm", swap_core)

    spread = jnp.broadcast_to(latent.reshape(2, 1, 64, C), (2, cols, 64, C)).reshape(-1, 64, C)
    frame = lax.all_to_all(spread, ("row", "col"), 0, 0, tiled=True)
    tiles = frame.reshape(2, cols, 8, 8, C)
    pick = lambda index: lax.dynamic_index_in_dim(tiles, index, 1, keepdims=False)
    before, own, after = (
        pick(jnp.maximum(col - 1, 0)),
        pick(col),
        pick(jnp.minimum(col + 1, cols - 1)),
    )
    empty = jnp.zeros((2, 8, 4, C), BF16)
    window = jnp.concatenate([before[:, :, 6:], own, after[:, :, :2], empty], axis=2)
    window = window.reshape(SPAN, C)
    slot = lax.rem(lax.broadcasted_iota(jnp.int32, (SPAN, 1), 0), SLOTS)
    column = col * 8 + slot - 2
    inside = (column >= 0) & (column < cols * 8)
    wide_frame = frame.reshape(-1, C).astype(F32)
    normed = (wide_frame * norm_factor(wide_frame) * norm_gain).astype(BF16)
    keys = jnp.dot(normed, w_key, preferred_element_type=F32).astype(BF16)
    values = jnp.dot(normed, w_value, preferred_element_type=F32).astype(BF16)
    wide_window = window.astype(F32)
    normed_window = (wide_window * norm_factor(wide_window) * norm_gain).astype(BF16)
    queries = jnp.dot(normed_window, w_query, preferred_element_type=F32).astype(BF16)
    scores = jnp.einsum("kd,qd->kq", keys, queries, preferred_element_type=F32) * inverse_root
    prob = jax.nn.softmax(scores, axis=0)
    context = jnp.einsum(
        "kq,kd->qd", prob.astype(BF16), values, preferred_element_type=F32
    ).astype(BF16)
    mixed = (wide_window + jnp.dot(context, w_out, preferred_element_type=F32)).astype(BF16)
    wide_mixed = mixed.astype(F32)
    act_one = jax.nn.silu(wide_mixed * norm_factor(wide_mixed) * gain_one)
    act_one = jnp.where(inside & (slot < 12), act_one, 0.0).astype(BF16)
    query_key = lax.dot_general(queries, w_key, NT, preferred_element_type=F32).astype(BF16)

    def framed(f0, f1, f2):
        stacked = jnp.stack([f.reshape(ROWS, SLOTS, C) for f in (f0, f1, f2)])
        return jnp.pad(stacked, ((0, 0), (1, 1), (0, 0), (0, 0)))

    act_frames = framed(moved(act_one, 2), moved(act_one, 1), act_one)

    keep = lax.dynamic_index_in_dim(grad_out, row, 0, keepdims=False)
    give = lax.dynamic_index_in_dim(grad_out, 1 - row, 0, keepdims=False)
    got = lax.ppermute(give, "row", swap_row)
    tile = jnp.concatenate([jnp.where(row == 0, keep, got), jnp.where(row == 0, got, keep)], axis=0)
    to_right = [(i, i + 1) for i in range(cols - 1)]
    to_left = [(i + 1, i) for i in range(cols - 1)]
    grad = jnp.concatenate(
        [
            lax.ppermute(tile[:, 6:], "col", to_right),
            tile,
            lax.ppermute(tile[:, :2], "col", to_left),
            jnp.zeros((ROWS, 4, C), BF16),
        ],
        axis=1,
    ).reshape(SPAN, C)
    grad_frames = framed(grad, moved(grad, -1), moved(grad, -2))

    ours = jnp.where(core == 0, act_frames, grad_frames)
    theirs = lax.ppermute(jnp.where(core == 0, grad_frames, act_frames), "tm", swap_core)
    both = jnp.stack([ours, theirs], axis=2).reshape(3, (ROWS + 2) * 2 * SLOTS, C)
    sums = pair_conv(core_arg, both, mine).reshape(ROWS, 2, SLOTS, C)
    kept = sums[:, 0].reshape(SPAN, C)
    given = lax.ppermute(sums[:, 1].reshape(SPAN, C), "tm", swap_core)
    conv_one = jnp.where(core == 0, kept, given).astype(BF16)
    g_act_two = jnp.where(core == 0, given, kept)
    wide_conv = conv_one.astype(F32)
    pre_two = wide_conv * norm_factor(wide_conv) * gain_two
    g_conv = norm_backward(wide_conv, gain_two, g_act_two * silu_slope(pre_two))
    g_conv = jnp.where(inside & (slot >= 1) & (slot < 11), g_conv, 0.0).astype(BF16)
    conv_frames = framed(g_conv, moved(g_conv, -1), moved(g_conv, -2))
    g_mixed = back_conv(
        core_arg,
        conv_frames.reshape(3, (ROWS + 2) * SLOTS, C),
        mine,
        other,
        grad,
        mixed,
        gain_one.reshape(1, C),
    )
    partial = attend_back(
        col_arg, g_mixed, prob, keys, values, query_key, w_out, w_value, w_query
    )
    parts = lax.all_to_all(partial.reshape(-1, 64, C), ("row", "col"), 0, 0, tiled=True)
    g_normed = jnp.sum(parts.reshape(2, cols, 64, C).astype(F32), axis=1).reshape(latent.shape)

    halves = g_mixed.reshape(2, 8, SLOTS, C)[:, :, 2:10]
    stay = lax.dynamic_index_in_dim(halves, row, 0, keepdims=False)
    leave = lax.dynamic_index_in_dim(halves, 1 - row, 0, keepdims=False)
    come = lax.ppermute(leave, "row", swap_row)
    g_tile = jnp.stack([jnp.where(row == 0, stay, come), jnp.where(row == 0, come, stay)])
    wide_latent = latent.astype(F32)
    return g_tile.astype(F32) + norm_backward(wide_latent, norm_gain, g_normed)


def solution(mesh):
    placed = (
        P("tm", "row", "col", None),
        P("tm", "row", "col", None),
        P(),
        P(),
        P(),
        P(),
        P(),
        P(),
        P(),
        P(None, None, None, "col", None),
        P(None, None, None, "col", None),
    )
    return jax.shard_map(
        shards, mesh=mesh, in_specs=placed, out_specs=P("tm", "row", "col", None), check_vma=False
    )
```

```python
import math

import jax
import jax.numpy as jnp
from jax import lax
from jax.experimental import pallas as pl
from jax.experimental.pallas import tpu as pltpu
from jax.sharding import PartitionSpec as P

EPSILON = 1e-06
F32, BF16 = jnp.float32, jnp.bfloat16
C = 384
ROWS, SLOTS = 16, 16
SPAN = ROWS * SLOTS
TILE = ROWS * 8
VMEM = 50 * 1024 * 1024
NT = (((1,), (1,)), ((), ()))


def norm_factor(field):
    return lax.rsqrt(jnp.mean(field * field, axis=-1, keepdims=True) + EPSILON)


def norm_backward(field, gain, upstream):
    factor = norm_factor(field)
    gained = gain * upstream
    return factor * gained - field * factor**3 * jnp.mean(field * gained, axis=-1, keepdims=True)


def silu_slope(pre):
    sig = jax.nn.sigmoid(pre)
    return sig * (1.0 + pre * (1.0 - sig))


def stage_shifts(x_ref, s_ref):
    length = x_ref.shape[1]
    for frame in range(3):
        wide = x_ref[frame].astype(F32)
        s_ref[frame, :, :C] = pltpu.roll(wide, 1, 0).astype(BF16)
        s_ref[frame, :, C : 2 * C] = x_ref[frame]
        s_ref[frame, :, 2 * C :] = pltpu.roll(wide, length - 1, 0).astype(BF16)


def fetch(core, mine_ref, other_ref, w_ref, sem, begin):
    count = w_ref.shape[0] // 3

    def copy(source, triple):
        return pltpu.make_async_copy(
            source.at[pl.ds(3 * (begin + triple), 3)], w_ref.at[pl.ds(3 * triple, 3)], sem.at[triple]
        )

    for triple in range(count):
        if other_ref is None:
            copy(mine_ref, triple).start()
        else:
            pl.when(core == 0)(lambda triple=triple: copy(mine_ref, triple).start())
            pl.when(core != 0)(lambda triple=triple: copy(other_ref, triple).start())
    return lambda triple: copy(mine_ref, triple).wait()


def pair_kernel(core_ref, x_ref, mine_ref, out_ref, s_ref, w_ref, sem):
    pitch, span = 2 * SLOTS, 2 * SPAN
    arrived = fetch(None, mine_ref, None, w_ref, sem, 0)
    stage_shifts(x_ref, s_ref)
    out_ref[...] = jnp.zeros_like(out_ref)
    for triple in range(9):
        arrived(triple)
        depth, down = triple // 3, triple % 3

        @pl.when(core_ref[0] == 0)
        def _():
            window = s_ref[depth, down * pitch : down * pitch + span, :]
            matrix = w_ref[3 * triple : 3 * triple + 3].reshape(3 * C, C)
            out_ref[...] += jnp.dot(window, matrix, preferred_element_type=F32)

        @pl.when(core_ref[0] != 0)
        def _():
            start = (2 - down) * pitch
            total = out_ref[...]
            for across in range(3):
                lane = (2 - across) * C
                window = s_ref[2 - depth, start : start + span, lane : lane + C]
                total += lax.dot_general(
                    window, w_ref[3 * triple + across], NT, preferred_element_type=F32
                )
            out_ref[...] = total


def pair_conv(core, x, mine):
    vmem = pl.BlockSpec(memory_space=pltpu.VMEM)
    return pl.pallas_call(
        pair_kernel,
        out_shape=jax.ShapeDtypeStruct((2 * SPAN, C), F32),
        in_specs=[pl.BlockSpec(memory_space=pltpu.SMEM), vmem, pl.BlockSpec(memory_space=pl.ANY)],
        out_specs=vmem,
        scratch_shapes=[
            pltpu.VMEM((3, x.shape[1], 3 * C), BF16),
            pltpu.VMEM((27, C, C), BF16),
            pltpu.SemaphoreType.DMA((9,)),
        ],
        compiler_params=pltpu.CompilerParams(vmem_limit_bytes=VMEM),
        cost_estimate=pl.CostEstimate(
            flops=2 * 27 * 2 * SPAN * C * C, bytes_accessed=27 * C * C * 2, transcendentals=0
        ),
        name="pair_conv",
    )(core, x, mine)


def back_kernel(depths, core_ref, *refs):
    count = len(depths)
    frame_refs, (mine_ref, other_ref), rest = refs[:count], refs[count : count + 2], refs[count + 2 :]
    if count == 2:
        start_ref, grad_ref, mixed_ref, gain_ref, out_ref, s_ref, wide_ref, tile_ref, w_ref, sem = rest
    else:
        out_ref, s_ref, wide_ref, tile_ref, w_ref, sem = rest
    arrived = fetch(core_ref[0], mine_ref, other_ref, w_ref, sem, 3 * depths[0])
    tile_ref[:, :8, :] = jnp.zeros((3, 8, C), F32)
    tile_ref[:, 8 + TILE :, :] = jnp.zeros((3, 8, C), F32)
    for place, frame_ref in enumerate(frame_refs):
        wide_ref[...] = frame_ref[...].astype(F32)
        for shift in range(3):
            for r in range(ROWS):
                tile_ref[shift, 8 + r * 8 : 16 + r * 8, :] = wide_ref[
                    r * 10 + shift : r * 10 + shift + 8, :
                ]
            for down in range(3):
                s_ref[place, down, :, shift * C : (shift + 1) * C] = tile_ref[
                    shift, down * 8 : down * 8 + TILE, :
                ].astype(BF16)
    total = start_ref[...] if count == 2 else jnp.zeros((TILE, C), F32)
    for triple in range(3 * count):
        arrived(triple)
        place, down = triple // 3, triple % 3
        for across in range(3):
            lane = (2 - across) * C
            window = s_ref[place, 2 - down, :, lane : lane + C]
            total += lax.dot_general(
                window, w_ref[3 * triple + across], NT, preferred_element_type=F32
            )
    if count == 2:
        mixed = mixed_ref[...].astype(F32)
        gain = gain_ref[...]
        slope = silu_slope(mixed * norm_factor(mixed) * gain)
        total = grad_ref[...].astype(F32) + norm_backward(mixed, gain, total * slope)
    out_ref[...] = total.astype(out_ref.dtype)


def back_conv(depths, core, frames, weights, rest=()):
    count = len(depths)
    vmem, remain = pl.BlockSpec(memory_space=pltpu.VMEM), pl.BlockSpec(memory_space=pl.ANY)
    return pl.pallas_call(
        lambda *refs: back_kernel(depths, *refs),
        out_shape=jax.ShapeDtypeStruct((TILE, C), BF16 if rest else F32),
        in_specs=[pl.BlockSpec(memory_space=pltpu.SMEM)]
        + [vmem] * count
        + [remain] * 2
        + [vmem] * len(rest),
        out_specs=vmem,
        scratch_shapes=[
            pltpu.VMEM((count, 3, TILE, 3 * C), BF16),
            pltpu.VMEM((ROWS * 10, C), F32),
            pltpu.VMEM((3, TILE + 16, C), F32),
            pltpu.VMEM((9 * count, C, C), BF16),
            pltpu.SemaphoreType.DMA((3 * count,)),
        ],
        compiler_params=pltpu.CompilerParams(vmem_limit_bytes=VMEM),
        cost_estimate=pl.CostEstimate(
            flops=2 * 9 * count * TILE * C * C, bytes_accessed=9 * count * C * C * 2, transcendentals=0
        ),
        name="back_conv",
    )(core, *frames, *weights, *rest)


CHUNK = 512


def attend_back_kernel(
    col_ref, gm_ref, prob_ref, keys_ref, values_ref, qk_ref, w_out_ref, w_value_ref, w_query_ref,
    out_ref, gp_ref, sum_ref, mix_ref, right_ref,
):
    positions = keys_ref.shape[0]
    count = positions // CHUNK
    inverse_root = 1.0 / math.sqrt(C)
    g_context = lax.dot_general(
        gm_ref[...], w_out_ref[...], NT, preferred_element_type=F32
    ).astype(BF16)
    right_ref[:TILE, :] = qk_ref[...]
    right_ref[TILE:, :] = lax.dot_general(
        g_context, w_value_ref[...], NT, preferred_element_type=F32
    ).astype(BF16)
    delta = jnp.zeros((1, TILE), F32)
    for c in range(count):
        part = pl.ds(c * CHUNK, CHUNK)
        g_prob = lax.dot_general(values_ref[part, :], g_context, NT, preferred_element_type=F32)
        gp_ref[part, :] = g_prob
        delta = delta + jnp.sum(prob_ref[part, :] * g_prob, axis=0, keepdims=True)
    g_query = jnp.zeros((TILE, C), F32)
    for c in range(count):
        part = pl.ds(c * CHUNK, CHUNK)
        prob = prob_ref[part, :]
        g_score = (prob * (gp_ref[part, :] - delta) * inverse_root).astype(BF16)
        mix_ref[:, :TILE] = g_score
        mix_ref[:, TILE:] = prob.astype(BF16)
        sum_ref[part, :] = jnp.dot(mix_ref[...], right_ref[...], preferred_element_type=F32)
        g_query += lax.dot_general(
            g_score, keys_ref[part, :], (((0,), (0,)), ((), ())), preferred_element_type=F32
        )
    high = g_query.astype(BF16)
    low = (g_query - high.astype(F32)).astype(BF16)
    local = lax.dot_general(high, w_query_ref[...], NT, preferred_element_type=F32)
    local += lax.dot_general(low, w_query_ref[...], NT, preferred_element_type=F32)
    for half in range(2):
        start = pl.multiple_of(half * (positions // 2) + col_ref[0] * 64, 64)
        sum_ref[pl.ds(start, 64), :] += local[half * 64 : half * 64 + 64]
    out_ref[...] = sum_ref[...].astype(BF16)


def attend_back(col, gm, prob, keys, values, qk, w_out, w_value, w_query):
    positions = keys.shape[0]
    return pl.pallas_call(
        attend_back_kernel,
        out_shape=jax.ShapeDtypeStruct((positions, C), BF16),
        in_specs=[pl.BlockSpec(memory_space=pltpu.SMEM)] + [pl.BlockSpec(memory_space=pltpu.VMEM)] * 8,
        out_specs=pl.BlockSpec(memory_space=pltpu.VMEM),
        scratch_shapes=[
            pltpu.VMEM((positions, TILE), F32),
            pltpu.VMEM((positions, C), F32),
            pltpu.VMEM((CHUNK, 2 * TILE), BF16),
            pltpu.VMEM((2 * TILE, C), BF16),
        ],
        compiler_params=pltpu.CompilerParams(vmem_limit_bytes=VMEM),
        cost_estimate=pl.CostEstimate(
            flops=10 * positions * TILE * C, bytes_accessed=8 * positions * C, transcendentals=0
        ),
        name="attend_back",
    )(col, gm, prob, keys, values, qk, w_out, w_value, w_query)


def shards(
    latent,
    grad_out,
    norm_gain,
    w_query,
    w_key,
    w_value,
    w_out,
    gain_one,
    gain_two,
    kernel_one,
    kernel_two,
):
    time_row = ("tm", "row")
    tm, row, col = lax.axis_index("tm"), lax.axis_index("row"), lax.axis_index("col")
    groups, cols = lax.axis_size("tm"), lax.axis_size("col")
    frames = groups * 2
    core = lax.rem(tm, 2)
    core_arg, col_arg = core.reshape(1), col.reshape(1)
    inverse_root = 1.0 / math.sqrt(C)
    swap_core = [(i, i ^ 1) for i in range(groups)]
    swap_row = [(0, 1), (1, 0)]

    def moved(value, steps):
        pairs = [(s, s + steps) for s in range(frames) if 0 <= s + steps < frames]
        return lax.ppermute(value, time_row, pairs)

    mine = lax.all_gather(
        jnp.where(core == 0, kernel_one, kernel_two), "col", axis=3, tiled=True
    ).reshape(27, C, C)

    spread = jnp.broadcast_to(latent.reshape(2, 1, 64, C), (2, cols, 64, C)).reshape(-1, 64, C)
    frame = lax.all_to_all(spread, ("row", "col"), 0, 0, tiled=True)
    tiles = frame.reshape(2, cols, 8, 8, C)
    pick = lambda index: lax.dynamic_index_in_dim(tiles, index, 1, keepdims=False)
    before, own, after = (
        pick(jnp.maximum(col - 1, 0)),
        pick(col),
        pick(jnp.minimum(col + 1, cols - 1)),
    )
    empty = jnp.zeros((2, 8, 4, C), BF16)
    window = jnp.concatenate([before[:, :, 6:], own, after[:, :, :2], empty], axis=2)
    window = window.reshape(SPAN, C)
    slot = lax.rem(lax.broadcasted_iota(jnp.int32, (SPAN, 1), 0), SLOTS)
    column = col * 8 + slot - 2
    inside = (column >= 0) & (column < cols * 8)
    wide_frame = frame.reshape(-1, C).astype(F32)
    normed = (wide_frame * norm_factor(wide_frame) * norm_gain).astype(BF16)
    keys = jnp.dot(normed, w_key, preferred_element_type=F32).astype(BF16)
    values = jnp.dot(normed, w_value, preferred_element_type=F32).astype(BF16)
    wide_window = window.astype(F32)
    normed_window = (wide_window * norm_factor(wide_window) * norm_gain).astype(BF16)
    queries = jnp.dot(normed_window, w_query, preferred_element_type=F32).astype(BF16)
    scores = jnp.einsum("kd,qd->kq", keys, queries, preferred_element_type=F32) * inverse_root
    prob = jax.nn.softmax(scores, axis=0)
    context = jnp.einsum(
        "kq,kd->qd", prob.astype(BF16), values, preferred_element_type=F32
    ).astype(BF16)
    mixed = (wide_window + jnp.dot(context, w_out, preferred_element_type=F32)).astype(BF16)
    wide_mixed = mixed.astype(F32)
    act_one = jax.nn.silu(wide_mixed * norm_factor(wide_mixed) * gain_one)
    act_one = jnp.where(inside & (slot < 12), act_one, 0.0).astype(BF16)

    def own_columns(value):
        return value.reshape(ROWS, SLOTS, C)[:, 2:10].reshape(TILE, C)

    own_queries = own_columns(queries)
    own_scores = jnp.einsum("kd,qd->kq", keys, own_queries, preferred_element_type=F32)
    own_prob = jax.nn.softmax(own_scores * inverse_root, axis=0)
    query_key = lax.dot_general(own_queries, w_key, NT, preferred_element_type=F32).astype(BF16)

    def framed(f0, f1, f2):
        stacked = jnp.stack([f.reshape(ROWS, SLOTS, C) for f in (f0, f1, f2)])
        return jnp.pad(stacked, ((0, 0), (1, 1), (0, 0), (0, 0)))

    act_frames = framed(moved(act_one, 2), moved(act_one, 1), act_one)

    keep = lax.dynamic_index_in_dim(grad_out, row, 0, keepdims=False)
    give = lax.dynamic_index_in_dim(grad_out, 1 - row, 0, keepdims=False)
    got = lax.ppermute(give, "row", swap_row)
    tile = jnp.concatenate([jnp.where(row == 0, keep, got), jnp.where(row == 0, got, keep)], axis=0)
    to_right = [(i, i + 1) for i in range(cols - 1)]
    to_left = [(i + 1, i) for i in range(cols - 1)]
    grad = jnp.concatenate(
        [
            lax.ppermute(tile[:, 6:], "col", to_right),
            tile,
            lax.ppermute(tile[:, :2], "col", to_left),
            jnp.zeros((ROWS, 4, C), BF16),
        ],
        axis=1,
    ).reshape(SPAN, C)
    grad_frames = framed(grad, moved(grad, -1), moved(grad, -2))

    ours = jnp.where(core == 0, act_frames, grad_frames)
    theirs = lax.ppermute(jnp.where(core == 0, grad_frames, act_frames), "tm", swap_core)
    both = jnp.stack([ours, theirs], axis=2).reshape(3, (ROWS + 2) * 2 * SLOTS, C)
    both, mine, own_prob, query_key = lax.optimization_barrier((both, mine, own_prob, query_key))
    other = lax.ppermute(mine, "tm", swap_core)
    sums = pair_conv(core_arg, both, mine).reshape(ROWS, 2, SLOTS, C)
    kept = sums[:, 0].reshape(SPAN, C)
    given = lax.ppermute(sums[:, 1].reshape(SPAN, C), "tm", swap_core)
    conv_one = jnp.where(core == 0, kept, given).astype(BF16)
    g_act_two = jnp.where(core == 0, given, kept)
    wide_conv = conv_one.astype(F32)
    pre_two = wide_conv * norm_factor(wide_conv) * gain_two
    g_conv = norm_backward(wide_conv, gain_two, g_act_two * silu_slope(pre_two))
    g_conv = jnp.where(inside, g_conv, 0.0).astype(BF16)
    g_conv = g_conv.reshape(ROWS, SLOTS, C)[:, 1:11].reshape(ROWS * 10, C)
    later = [moved(g_conv, -2), moved(g_conv, -1)]
    weights = (mine, other)
    own_part = back_conv((2,), core_arg, [g_conv], weights)
    rest = (own_part, own_columns(grad), own_columns(mixed), gain_one.reshape(1, C))
    g_mixed = back_conv((0, 1), core_arg, later, weights, rest)

    halves = g_mixed.reshape(2, 8, 8, C)
    stay = lax.dynamic_index_in_dim(halves, row, 0, keepdims=False)
    leave = lax.dynamic_index_in_dim(halves, 1 - row, 0, keepdims=False)
    come = lax.ppermute(leave, "row", swap_row)
    g_tile = jnp.stack([jnp.where(row == 0, stay, come), jnp.where(row == 0, come, stay)])
    partial = attend_back(
        col_arg, g_mixed, own_prob, keys, values, query_key, w_out, w_value, w_query
    )
    partial, g_tile = lax.optimization_barrier((partial, g_tile))
    parts = lax.all_to_all(partial.reshape(-1, 64, C), ("row", "col"), 0, 0, tiled=True)
    g_normed = jnp.sum(parts.reshape(2, cols, 64, C).astype(F32), axis=1).reshape(latent.shape)

    wide_latent = latent.astype(F32)
    return g_tile.astype(F32) + norm_backward(wide_latent, norm_gain, g_normed)


def solution(mesh):
    placed = (
        P("tm", "row", "col", None),
        P("tm", "row", "col", None),
        P(),
        P(),
        P(),
        P(),
        P(),
        P(),
        P(),
        P(None, None, None, "col", None),
        P(None, None, None, "col", None),
    )
    return jax.shard_map(
        shards, mesh=mesh, in_specs=placed, out_specs=P("tm", "row", "col", None), check_vma=False
    )
```

```python
import math

import jax
import jax.numpy as jnp
from jax import lax
from jax.experimental import pallas as pl
from jax.experimental.pallas import tpu as pltpu
from jax.sharding import PartitionSpec as P

EPSILON = 1e-06
F32, BF16 = jnp.float32, jnp.bfloat16
C = 384
ROWS, SLOTS = 16, 16
SPAN = ROWS * SLOTS
TILE = ROWS * 8
VMEM = 50 * 1024 * 1024
NT = (((1,), (1,)), ((), ()))


def norm_factor(field):
    return lax.rsqrt(jnp.mean(field * field, axis=-1, keepdims=True) + EPSILON)


def norm_backward(field, gain, upstream):
    factor = norm_factor(field)
    gained = gain * upstream
    return factor * gained - field * factor**3 * jnp.mean(field * gained, axis=-1, keepdims=True)


def silu_slope(pre):
    sig = jax.nn.sigmoid(pre)
    return sig * (1.0 + pre * (1.0 - sig))


def stage_shifts(x_ref, s_ref):
    length = x_ref.shape[1]
    for frame in range(3):
        wide = x_ref[frame].astype(F32)
        s_ref[frame, :, :C] = pltpu.roll(wide, 1, 0).astype(BF16)
        s_ref[frame, :, C : 2 * C] = x_ref[frame]
        s_ref[frame, :, 2 * C :] = pltpu.roll(wide, length - 1, 0).astype(BF16)


def fetch(core, mine_ref, other_ref, w_ref, sem, begin):
    count = w_ref.shape[0] // 3

    def copy(source, triple):
        return pltpu.make_async_copy(
            source.at[pl.ds(3 * (begin + triple), 3)], w_ref.at[pl.ds(3 * triple, 3)], sem.at[triple]
        )

    for triple in range(count):
        if other_ref is None:
            copy(mine_ref, triple).start()
        else:
            pl.when(core == 0)(lambda triple=triple: copy(mine_ref, triple).start())
            pl.when(core != 0)(lambda triple=triple: copy(other_ref, triple).start())
    return lambda triple: copy(mine_ref, triple).wait()


def pair_kernel(core_ref, x_ref, mine_ref, out_ref, s_ref, w_ref, sem):
    pitch, span = 2 * SLOTS, 2 * SPAN
    arrived = fetch(None, mine_ref, None, w_ref, sem, 0)
    stage_shifts(x_ref, s_ref)

    def windows(depth, down, lanes):
        return s_ref[depth, down * pitch : down * pitch + span, lanes]

    for depth in range(3):
        for down in range(3):
            arrived(3 * depth + down)
        taps = range(9 * depth, 9 * depth + 9)

        def add(term, depth=depth):
            out_ref[...] = term if depth == 0 else out_ref[...] + term

        @pl.when(core_ref[0] == 0)
        def _():
            window = jnp.concatenate(
                [windows(depth, down, slice(0, 3 * C)) for down in range(3)], axis=1
            )
            matrix = w_ref[9 * depth : 9 * depth + 9].reshape(9 * C, C)
            add(jnp.dot(window, matrix, preferred_element_type=F32))

        @pl.when(core_ref[0] != 0)
        def _():
            window = jnp.concatenate(
                [
                    windows(2 - depth, 2 - down, slice((2 - across) * C, (3 - across) * C))
                    for down in range(3)
                    for across in range(3)
                ],
                axis=1,
            )
            matrix = jnp.concatenate([w_ref[tap] for tap in taps], axis=1)
            add(lax.dot_general(window, matrix, NT, preferred_element_type=F32))


def pair_conv(core, x, mine):
    vmem = pl.BlockSpec(memory_space=pltpu.VMEM)
    return pl.pallas_call(
        pair_kernel,
        out_shape=jax.ShapeDtypeStruct((2 * SPAN, C), F32),
        in_specs=[pl.BlockSpec(memory_space=pltpu.SMEM), vmem, pl.BlockSpec(memory_space=pl.ANY)],
        out_specs=vmem,
        scratch_shapes=[
            pltpu.VMEM((3, x.shape[1], 3 * C), BF16),
            pltpu.VMEM((27, C, C), BF16),
            pltpu.SemaphoreType.DMA((9,)),
        ],
        compiler_params=pltpu.CompilerParams(vmem_limit_bytes=VMEM),
        cost_estimate=pl.CostEstimate(
            flops=2 * 27 * 2 * SPAN * C * C, bytes_accessed=27 * C * C * 2, transcendentals=0
        ),
        name="pair_conv",
    )(core, x, mine)


def window_of(frame_ref, place, s_ref, wide_ref, tile_ref):
    wide_ref[...] = frame_ref[...].astype(F32)
    for shift in range(3):
        for r in range(ROWS):
            tile_ref[shift, 8 + r * 8 : 16 + r * 8, :] = wide_ref[
                r * 10 + shift : r * 10 + shift + 8, :
            ]
        for down in range(3):
            s_ref[place, down, :, shift * C : (shift + 1) * C] = tile_ref[
                shift, down * 8 : down * 8 + TILE, :
            ].astype(BF16)


def back_taps(frame_refs, arrived, s_ref, wide_ref, tile_ref, w_ref, total):
    tile_ref[:, :8, :] = jnp.zeros((3, 8, C), F32)
    tile_ref[:, 8 + TILE :, :] = jnp.zeros((3, 8, C), F32)
    for place, frame_ref in enumerate(frame_refs):
        window_of(frame_ref, place, s_ref, wide_ref, tile_ref)
    for triple in range(3 * len(frame_refs)):
        arrived(triple)
        place, down = triple // 3, triple % 3
        for across in range(3):
            lane = (2 - across) * C
            window = s_ref[place, 2 - down, :, lane : lane + C]
            total += lax.dot_general(
                window, w_ref[3 * triple + across], NT, preferred_element_type=F32
            )
    return total


def own_kernel(core_ref, frame_ref, mine_ref, other_ref, out_ref, s_ref, wide_ref, tile_ref, w_ref, sem):
    arrived = fetch(core_ref[0], mine_ref, other_ref, w_ref, sem, 6)
    zero = jnp.zeros((TILE, C), F32)
    out_ref[...] = back_taps([frame_ref], arrived, s_ref, wide_ref, tile_ref, w_ref, zero)


def back_scratch(count):
    return [
        pltpu.VMEM((count, 3, TILE, 3 * C), BF16),
        pltpu.VMEM((ROWS * 10, C), F32),
        pltpu.VMEM((3, TILE + 16, C), F32),
        pltpu.VMEM((9 * count, C, C), BF16),
        pltpu.SemaphoreType.DMA((3 * count,)),
    ]


def back_own(core, frame, mine, other):
    smem, vmem = pl.BlockSpec(memory_space=pltpu.SMEM), pl.BlockSpec(memory_space=pltpu.VMEM)
    remain = pl.BlockSpec(memory_space=pl.ANY)
    return pl.pallas_call(
        own_kernel,
        out_shape=jax.ShapeDtypeStruct((TILE, C), F32),
        in_specs=[smem, vmem, remain, remain],
        out_specs=vmem,
        scratch_shapes=back_scratch(1),
        compiler_params=pltpu.CompilerParams(vmem_limit_bytes=VMEM),
        cost_estimate=pl.CostEstimate(
            flops=2 * 9 * TILE * C * C, bytes_accessed=9 * C * C * 2, transcendentals=0
        ),
        name="back_own",
    )(core, frame, mine, other)


CHUNK = 512


def back_kernel(
    core_ref, col_ref, late_ref, soon_ref, mine_ref, other_ref, start_ref, grad_ref, mixed_ref, gain_ref,
    qk_ref, w_out_ref, w_value_ref, w_query_ref, prob_from, keys_from, values_from,
    gm_ref, out_ref,
    s_ref, wide_ref, tile_ref, w_ref, sem, prob_ref, keys_ref, values_ref, in_sem,
    gp_ref, sum_ref, mix_ref, right_ref,
):
    arrived = fetch(core_ref[0], mine_ref, other_ref, w_ref, sem, 0)
    pairs = ((values_from, values_ref), (prob_from, prob_ref), (keys_from, keys_ref))
    inputs = [
        pltpu.make_async_copy(source, target, in_sem.at[i])
        for i, (source, target) in enumerate(pairs)
    ]
    for copy in inputs:
        copy.start()
    total = back_taps(
        [late_ref, soon_ref], arrived, s_ref, wide_ref, tile_ref, w_ref, start_ref[...]
    )
    mixed = mixed_ref[...].astype(F32)
    gain = gain_ref[...]
    slope = silu_slope(mixed * norm_factor(mixed) * gain)
    total = grad_ref[...].astype(F32) + norm_backward(mixed, gain, total * slope)
    g_mixed = total.astype(BF16)
    gm_ref[...] = g_mixed

    positions = keys_ref.shape[0]
    count = positions // CHUNK
    inverse_root = 1.0 / math.sqrt(C)
    g_context = lax.dot_general(g_mixed, w_out_ref[...], NT, preferred_element_type=F32)
    g_context = g_context.astype(BF16)
    right_ref[:TILE, :] = qk_ref[...]
    right_ref[TILE:, :] = lax.dot_general(
        g_context, w_value_ref[...], NT, preferred_element_type=F32
    ).astype(BF16)
    for copy in inputs:
        copy.wait()
    delta = jnp.zeros((1, TILE), F32)
    for c in range(count):
        part = pl.ds(c * CHUNK, CHUNK)
        g_prob = lax.dot_general(values_ref[part, :], g_context, NT, preferred_element_type=F32)
        gp_ref[part, :] = g_prob
        delta = delta + jnp.sum(prob_ref[part, :] * g_prob, axis=0, keepdims=True)
    g_query = jnp.zeros((TILE, C), F32)
    for c in range(count):
        part = pl.ds(c * CHUNK, CHUNK)
        prob = prob_ref[part, :]
        g_score = (prob * (gp_ref[part, :] - delta) * inverse_root).astype(BF16)
        mix_ref[:, :TILE] = g_score
        mix_ref[:, TILE:] = prob.astype(BF16)
        sum_ref[part, :] = jnp.dot(mix_ref[...], right_ref[...], preferred_element_type=F32)
        g_query += lax.dot_general(
            g_score, keys_ref[part, :], (((0,), (0,)), ((), ())), preferred_element_type=F32
        )
    high = g_query.astype(BF16)
    low = (g_query - high.astype(F32)).astype(BF16)
    local = lax.dot_general(high, w_query_ref[...], NT, preferred_element_type=F32)
    local += lax.dot_general(low, w_query_ref[...], NT, preferred_element_type=F32)
    for half in range(2):
        start = pl.multiple_of(half * (positions // 2) + col_ref[0] * 64, 64)
        sum_ref[pl.ds(start, 64), :] += local[half * 64 : half * 64 + 64]
    out_ref[...] = sum_ref[...].astype(BF16)


def back_rest(core, col, frames, weights, conv_rest, small, large):
    positions = large[1].shape[0]
    smem, vmem = pl.BlockSpec(memory_space=pltpu.SMEM), pl.BlockSpec(memory_space=pltpu.VMEM)
    remain = pl.BlockSpec(memory_space=pl.ANY)
    return pl.pallas_call(
        back_kernel,
        out_shape=(
            jax.ShapeDtypeStruct((TILE, C), BF16),
            jax.ShapeDtypeStruct((positions, C), BF16),
        ),
        in_specs=[smem] * 2 + [vmem] * 2 + [remain] * 2 + [vmem] * 8 + [remain] * 3,
        out_specs=(vmem, vmem),
        scratch_shapes=back_scratch(2)
        + [
            pltpu.VMEM((positions, TILE), F32),
            pltpu.VMEM((positions, C), BF16),
            pltpu.VMEM((positions, C), BF16),
            pltpu.SemaphoreType.DMA((3,)),
            pltpu.VMEM((positions, TILE), F32),
            pltpu.VMEM((positions, C), F32),
            pltpu.VMEM((CHUNK, 2 * TILE), BF16),
            pltpu.VMEM((2 * TILE, C), BF16),
        ],
        compiler_params=pltpu.CompilerParams(vmem_limit_bytes=VMEM),
        cost_estimate=pl.CostEstimate(
            flops=2 * 18 * TILE * C * C + 10 * positions * TILE * C,
            bytes_accessed=18 * C * C * 2 + 8 * positions * C,
            transcendentals=0,
        ),
        name="back_rest",
    )(core, col, *frames, *weights, *conv_rest, *small, *large)


def shards(
    latent,
    grad_out,
    norm_gain,
    w_query,
    w_key,
    w_value,
    w_out,
    gain_one,
    gain_two,
    kernel_one,
    kernel_two,
):
    time_row = ("tm", "row")
    tm, row, col = lax.axis_index("tm"), lax.axis_index("row"), lax.axis_index("col")
    groups, cols = lax.axis_size("tm"), lax.axis_size("col")
    frames = groups * 2
    core = lax.rem(tm, 2)
    core_arg, col_arg = core.reshape(1), col.reshape(1)
    inverse_root = 1.0 / math.sqrt(C)
    swap_core = [(i, i ^ 1) for i in range(groups)]
    swap_row = [(0, 1), (1, 0)]

    def moved(value, steps):
        pairs = [(s, s + steps) for s in range(frames) if 0 <= s + steps < frames]
        return lax.ppermute(value, time_row, pairs)

    mine = lax.all_gather(
        jnp.where(core == 0, kernel_one, kernel_two), "col", axis=3, tiled=True
    ).reshape(27, C, C)

    spread = jnp.broadcast_to(latent.reshape(2, 1, 64, C), (2, cols, 64, C)).reshape(-1, 64, C)
    frame = lax.all_to_all(spread, ("row", "col"), 0, 0, tiled=True)
    tiles = frame.reshape(2, cols, 8, 8, C)
    pick = lambda index: lax.dynamic_index_in_dim(tiles, index, 1, keepdims=False)
    before, own, after = (
        pick(jnp.maximum(col - 1, 0)),
        pick(col),
        pick(jnp.minimum(col + 1, cols - 1)),
    )
    empty = jnp.zeros((2, 8, 4, C), BF16)
    window = jnp.concatenate([before[:, :, 6:], own, after[:, :, :2], empty], axis=2)
    window = window.reshape(SPAN, C)
    slot = lax.rem(lax.broadcasted_iota(jnp.int32, (SPAN, 1), 0), SLOTS)
    column = col * 8 + slot - 2
    inside = (column >= 0) & (column < cols * 8)
    wide_frame = frame.reshape(-1, C).astype(F32)
    normed = (wide_frame * norm_factor(wide_frame) * norm_gain).astype(BF16)
    keys = jnp.dot(normed, w_key, preferred_element_type=F32).astype(BF16)
    values = jnp.dot(normed, w_value, preferred_element_type=F32).astype(BF16)
    wide_window = window.astype(F32)
    normed_window = (wide_window * norm_factor(wide_window) * norm_gain).astype(BF16)
    queries = jnp.dot(normed_window, w_query, preferred_element_type=F32).astype(BF16)
    scores = jnp.einsum("kd,qd->kq", keys, queries, preferred_element_type=F32) * inverse_root
    prob = jax.nn.softmax(scores, axis=0)
    context = jnp.einsum(
        "kq,kd->qd", prob.astype(BF16), values, preferred_element_type=F32
    ).astype(BF16)
    mixed = (wide_window + jnp.dot(context, w_out, preferred_element_type=F32)).astype(BF16)
    wide_mixed = mixed.astype(F32)
    act_one = jax.nn.silu(wide_mixed * norm_factor(wide_mixed) * gain_one)
    act_one = jnp.where(inside & (slot < 12), act_one, 0.0).astype(BF16)

    def own_columns(value):
        return value.reshape(ROWS, SLOTS, C)[:, 2:10].reshape(TILE, C)

    own_queries = own_columns(queries)
    own_scores = jnp.einsum("kd,qd->kq", keys, own_queries, preferred_element_type=F32)
    own_prob = jax.nn.softmax(own_scores * inverse_root, axis=0)
    query_key = lax.dot_general(own_queries, w_key, NT, preferred_element_type=F32).astype(BF16)

    def framed(f0, f1, f2):
        stacked = jnp.stack([f.reshape(ROWS, SLOTS, C) for f in (f0, f1, f2)])
        return jnp.pad(stacked, ((0, 0), (1, 1), (0, 0), (0, 0)))

    act_frames = framed(moved(act_one, 2), moved(act_one, 1), act_one)

    keep = lax.dynamic_index_in_dim(grad_out, row, 0, keepdims=False)
    give = lax.dynamic_index_in_dim(grad_out, 1 - row, 0, keepdims=False)
    got = lax.ppermute(give, "row", swap_row)
    tile = jnp.concatenate([jnp.where(row == 0, keep, got), jnp.where(row == 0, got, keep)], axis=0)
    to_right = [(i, i + 1) for i in range(cols - 1)]
    to_left = [(i + 1, i) for i in range(cols - 1)]
    grad = jnp.concatenate(
        [
            lax.ppermute(tile[:, 6:], "col", to_right),
            tile,
            lax.ppermute(tile[:, :2], "col", to_left),
            jnp.zeros((ROWS, 4, C), BF16),
        ],
        axis=1,
    ).reshape(SPAN, C)
    grad_frames = framed(grad, moved(grad, -1), moved(grad, -2))

    ours = jnp.where(core == 0, act_frames, grad_frames)
    theirs = lax.ppermute(jnp.where(core == 0, grad_frames, act_frames), "tm", swap_core)
    both = jnp.stack([ours, theirs], axis=2).reshape(3, (ROWS + 2) * 2 * SLOTS, C)
    both, mine, own_prob, query_key = lax.optimization_barrier((both, mine, own_prob, query_key))
    other = lax.ppermute(mine, "tm", swap_core)
    sums = pair_conv(core_arg, both, mine).reshape(ROWS, 2, SLOTS, C)
    kept = sums[:, 0].reshape(SPAN, C)
    given = lax.ppermute(sums[:, 1].reshape(SPAN, C).astype(BF16), "tm", swap_core)
    conv_one = jnp.where(core == 0, kept.astype(BF16), given)
    g_act_two = jnp.where(core == 0, given.astype(F32), kept)
    wide_conv = conv_one.astype(F32)
    pre_two = wide_conv * norm_factor(wide_conv) * gain_two
    g_conv = norm_backward(wide_conv, gain_two, g_act_two * silu_slope(pre_two))
    g_conv = jnp.where(inside, g_conv, 0.0).astype(BF16)
    g_conv = g_conv.reshape(ROWS, SLOTS, C)[:, 1:11].reshape(ROWS * 10, C)
    later = [moved(g_conv, -2), moved(g_conv, -1)]
    own_part = back_own(core_arg, g_conv, mine, other)
    g_mixed, partial = back_rest(
        core_arg,
        col_arg,
        later,
        (mine, other),
        (own_part, own_columns(grad), own_columns(mixed), gain_one.reshape(1, C)),
        (query_key, w_out, w_value, w_query),
        (own_prob, keys, values),
    )

    halves = g_mixed.reshape(2, 8, 8, C)
    stay = lax.dynamic_index_in_dim(halves, row, 0, keepdims=False)
    leave = lax.dynamic_index_in_dim(halves, 1 - row, 0, keepdims=False)
    come = lax.ppermute(leave, "row", swap_row)
    g_tile = jnp.stack([jnp.where(row == 0, stay, come), jnp.where(row == 0, come, stay)])
    parts = lax.all_to_all(partial.reshape(-1, 64, C), ("row", "col"), 0, 0, tiled=True)
    g_normed = jnp.sum(parts.reshape(2, cols, 64, C).astype(F32), axis=1).reshape(latent.shape)

    wide_latent = latent.astype(F32)
    return g_tile.astype(F32) + norm_backward(wide_latent, norm_gain, g_normed)


def solution(mesh):
    placed = (
        P("tm", "row", "col", None),
        P("tm", "row", "col", None),
        P(),
        P(),
        P(),
        P(),
        P(),
        P(),
        P(),
        P(None, None, None, "col", None),
        P(None, None, None, "col", None),
    )
    return jax.shard_map(
        shards, mesh=mesh, in_specs=placed, out_specs=P("tm", "row", "col", None), check_vma=False
    )
```

```python
import math

import jax
import jax.numpy as jnp
from jax import lax
from jax.experimental import pallas as pl
from jax.experimental.pallas import tpu as pltpu
from jax.sharding import PartitionSpec as P

EPSILON = 1e-06
F32, BF16 = jnp.float32, jnp.bfloat16
C = 384
ROWS, SLOTS = 16, 16
SPAN = ROWS * SLOTS
TILE = ROWS * 8
VMEM = 50 * 1024 * 1024
NT = (((1,), (1,)), ((), ()))


def norm_factor(field):
    return lax.rsqrt(jnp.mean(field * field, axis=-1, keepdims=True) + EPSILON)


def norm_backward(field, gain, upstream):
    factor = norm_factor(field)
    gained = gain * upstream
    return factor * gained - field * factor**3 * jnp.mean(field * gained, axis=-1, keepdims=True)


def silu_slope(pre):
    sig = jax.nn.sigmoid(pre)
    return sig * (1.0 + pre * (1.0 - sig))


def stage_shifts(x_ref, s_ref, frame):
    length = x_ref.shape[1]
    wide = x_ref[frame].astype(F32)
    s_ref[frame, :, :C] = pltpu.roll(wide, 1, 0).astype(BF16)
    s_ref[frame, :, C : 2 * C] = x_ref[frame]
    s_ref[frame, :, 2 * C :] = pltpu.roll(wide, length - 1, 0).astype(BF16)


def fetch(core, mine_ref, other_ref, w_ref, sem, begin):
    count = w_ref.shape[0] // 3

    def copy(source, triple):
        return pltpu.make_async_copy(
            source.at[pl.ds(3 * (begin + triple), 3)], w_ref.at[pl.ds(3 * triple, 3)], sem.at[triple]
        )

    for triple in range(count):
        if other_ref is None:
            copy(mine_ref, triple).start()
        else:
            pl.when(core == 0)(lambda triple=triple: copy(mine_ref, triple).start())
            pl.when(core != 0)(lambda triple=triple: copy(other_ref, triple).start())
    return lambda triple: copy(mine_ref, triple).wait()


def pair_kernel(core_ref, x_ref, mine_ref, out_ref, s_ref, w_ref, sem):
    pitch, span = 2 * SLOTS, 2 * SPAN
    arrived = fetch(None, mine_ref, None, w_ref, sem, 0)

    def windows(depth, down, lanes):
        return s_ref[depth, down * pitch : down * pitch + span, lanes]

    def causal(depth):
        window = jnp.concatenate(
            [windows(depth, down, slice(0, 3 * C)) for down in range(3)], axis=1
        )
        matrix = w_ref[9 * depth : 9 * depth + 9].reshape(9 * C, C)
        return jnp.dot(window, matrix, preferred_element_type=F32)

    def transposed(depth):
        window = jnp.concatenate(
            [
                windows(2 - depth, 2 - down, slice((2 - across) * C, (3 - across) * C))
                for down in range(3)
                for across in range(3)
            ],
            axis=1,
        )
        matrix = jnp.concatenate([w_ref[9 * depth + tap] for tap in range(9)], axis=1)
        return lax.dot_general(window, matrix, NT, preferred_element_type=F32)

    def work(order, part):
        stage_shifts(x_ref, s_ref, order[0])
        for depth in range(3):
            for down in range(3):
                arrived(3 * depth + down)
            if depth < 2:
                stage_shifts(x_ref, s_ref, order[depth + 1])
            term = part(depth)
            out_ref[...] = term if depth == 0 else out_ref[...] + term

    pl.when(core_ref[0] == 0)(lambda: work((0, 1, 2), causal))
    pl.when(core_ref[0] != 0)(lambda: work((2, 1, 0), transposed))


def pair_conv(core, x, mine):
    vmem = pl.BlockSpec(memory_space=pltpu.VMEM)
    return pl.pallas_call(
        pair_kernel,
        out_shape=jax.ShapeDtypeStruct((2 * SPAN, C), F32),
        in_specs=[pl.BlockSpec(memory_space=pltpu.SMEM), vmem, pl.BlockSpec(memory_space=pl.ANY)],
        out_specs=vmem,
        scratch_shapes=[
            pltpu.VMEM((3, x.shape[1], 3 * C), BF16),
            pltpu.VMEM((27, C, C), BF16),
            pltpu.SemaphoreType.DMA((9,)),
        ],
        compiler_params=pltpu.CompilerParams(vmem_limit_bytes=VMEM),
        cost_estimate=pl.CostEstimate(
            flops=2 * 27 * 2 * SPAN * C * C, bytes_accessed=27 * C * C * 2, transcendentals=0
        ),
        name="pair_conv",
    )(core, x, mine)


def window_of(frame_ref, place, s_ref, wide_ref, tile_ref):
    wide_ref[...] = frame_ref[...].astype(F32)
    for shift in range(3):
        for r in range(ROWS):
            tile_ref[shift, 8 + r * 8 : 16 + r * 8, :] = wide_ref[
                r * 10 + shift : r * 10 + shift + 8, :
            ]
        for down in range(3):
            s_ref[place, down, :, shift * C : (shift + 1) * C] = tile_ref[
                shift, down * 8 : down * 8 + TILE, :
            ].astype(BF16)


def back_taps(frame_refs, arrived, s_ref, wide_ref, tile_ref, w_ref, total):
    tile_ref[:, :8, :] = jnp.zeros((3, 8, C), F32)
    tile_ref[:, 8 + TILE :, :] = jnp.zeros((3, 8, C), F32)
    for place, frame_ref in enumerate(frame_refs):
        window_of(frame_ref, place, s_ref, wide_ref, tile_ref)
    for triple in range(3 * len(frame_refs)):
        arrived(triple)
        place, down = triple // 3, triple % 3
        for across in range(3):
            lane = (2 - across) * C
            window = s_ref[place, 2 - down, :, lane : lane + C]
            total += lax.dot_general(
                window, w_ref[3 * triple + across], NT, preferred_element_type=F32
            )
    return total


def own_kernel(core_ref, frame_ref, mine_ref, other_ref, out_ref, s_ref, wide_ref, tile_ref, w_ref, sem):
    arrived = fetch(core_ref[0], mine_ref, other_ref, w_ref, sem, 6)
    zero = jnp.zeros((TILE, C), F32)
    out_ref[...] = back_taps([frame_ref], arrived, s_ref, wide_ref, tile_ref, w_ref, zero)


def back_scratch(count):
    return [
        pltpu.VMEM((count, 3, TILE, 3 * C), BF16),
        pltpu.VMEM((ROWS * 10, C), F32),
        pltpu.VMEM((3, TILE + 16, C), F32),
        pltpu.VMEM((9 * count, C, C), BF16),
        pltpu.SemaphoreType.DMA((3 * count,)),
    ]


def back_own(core, frame, mine, other):
    smem, vmem = pl.BlockSpec(memory_space=pltpu.SMEM), pl.BlockSpec(memory_space=pltpu.VMEM)
    remain = pl.BlockSpec(memory_space=pl.ANY)
    return pl.pallas_call(
        own_kernel,
        out_shape=jax.ShapeDtypeStruct((TILE, C), F32),
        in_specs=[smem, vmem, remain, remain],
        out_specs=vmem,
        scratch_shapes=back_scratch(1),
        compiler_params=pltpu.CompilerParams(vmem_limit_bytes=VMEM),
        cost_estimate=pl.CostEstimate(
            flops=2 * 9 * TILE * C * C, bytes_accessed=9 * C * C * 2, transcendentals=0
        ),
        name="back_own",
    )(core, frame, mine, other)


CHUNK = 512


def back_kernel(
    core_ref, col_ref, late_ref, soon_ref, mine_ref, other_ref, start_ref, grad_ref, mixed_ref, gain_ref,
    qk_ref, w_out_ref, w_value_ref, w_query_ref, prob_from, keys_from, values_from,
    gm_ref, out_ref,
    s_ref, wide_ref, tile_ref, w_ref, sem, prob_ref, keys_ref, values_ref, in_sem,
    gp_ref, sum_ref, mix_ref, right_ref,
):
    arrived = fetch(core_ref[0], mine_ref, other_ref, w_ref, sem, 0)
    pairs = ((values_from, values_ref), (prob_from, prob_ref), (keys_from, keys_ref))
    inputs = [
        pltpu.make_async_copy(source, target, in_sem.at[i])
        for i, (source, target) in enumerate(pairs)
    ]
    for copy in inputs:
        copy.start()
    total = back_taps(
        [late_ref, soon_ref], arrived, s_ref, wide_ref, tile_ref, w_ref, start_ref[...]
    )
    mixed = mixed_ref[...].astype(F32)
    gain = gain_ref[...]
    slope = silu_slope(mixed * norm_factor(mixed) * gain)
    total = grad_ref[...].astype(F32) + norm_backward(mixed, gain, total * slope)
    g_mixed = total.astype(BF16)
    gm_ref[...] = g_mixed

    positions = keys_ref.shape[0]
    count = positions // CHUNK
    inverse_root = 1.0 / math.sqrt(C)
    g_context = lax.dot_general(g_mixed, w_out_ref[...], NT, preferred_element_type=F32)
    g_context = g_context.astype(BF16)
    right_ref[:TILE, :] = qk_ref[...]
    right_ref[TILE:, :] = lax.dot_general(
        g_context, w_value_ref[...], NT, preferred_element_type=F32
    ).astype(BF16)
    for copy in inputs:
        copy.wait()
    delta = jnp.zeros((1, TILE), F32)
    for c in range(count):
        part = pl.ds(c * CHUNK, CHUNK)
        g_prob = lax.dot_general(values_ref[part, :], g_context, NT, preferred_element_type=F32)
        gp_ref[part, :] = g_prob
        delta = delta + jnp.sum(prob_ref[part, :] * g_prob, axis=0, keepdims=True)
    g_query = jnp.zeros((TILE, C), F32)
    for c in range(count):
        part = pl.ds(c * CHUNK, CHUNK)
        prob = prob_ref[part, :]
        g_score = (prob * (gp_ref[part, :] - delta) * inverse_root).astype(BF16)
        mix_ref[:, :TILE] = g_score
        mix_ref[:, TILE:] = prob.astype(BF16)
        sum_ref[part, :] = jnp.dot(mix_ref[...], right_ref[...], preferred_element_type=F32)
        g_query += lax.dot_general(
            g_score, keys_ref[part, :], (((0,), (0,)), ((), ())), preferred_element_type=F32
        )
    high = g_query.astype(BF16)
    low = (g_query - high.astype(F32)).astype(BF16)
    local = lax.dot_general(high, w_query_ref[...], NT, preferred_element_type=F32)
    local += lax.dot_general(low, w_query_ref[...], NT, preferred_element_type=F32)
    start = pl.multiple_of(col_ref[0] * TILE, TILE)
    sum_ref[pl.ds(start, TILE), :] += local
    tiles = positions // TILE
    for half in range(2):
        for tile in range(tiles):
            there, here = (half * tiles + tile) * 64, tile * TILE + half * 64
            out_ref[there : there + 64, :] = sum_ref[here : here + 64, :].astype(BF16)


def back_rest(core, col, frames, weights, conv_rest, small, large):
    positions = large[1].shape[0]
    smem, vmem = pl.BlockSpec(memory_space=pltpu.SMEM), pl.BlockSpec(memory_space=pltpu.VMEM)
    remain = pl.BlockSpec(memory_space=pl.ANY)
    return pl.pallas_call(
        back_kernel,
        out_shape=(
            jax.ShapeDtypeStruct((TILE, C), BF16),
            jax.ShapeDtypeStruct((positions, C), BF16),
        ),
        in_specs=[smem] * 2 + [vmem] * 2 + [remain] * 2 + [vmem] * 8 + [remain] * 3,
        out_specs=(vmem, vmem),
        scratch_shapes=back_scratch(2)
        + [
            pltpu.VMEM((positions, TILE), F32),
            pltpu.VMEM((positions, C), BF16),
            pltpu.VMEM((positions, C), BF16),
            pltpu.SemaphoreType.DMA((3,)),
            pltpu.VMEM((positions, TILE), F32),
            pltpu.VMEM((positions, C), F32),
            pltpu.VMEM((CHUNK, 2 * TILE), BF16),
            pltpu.VMEM((2 * TILE, C), BF16),
        ],
        compiler_params=pltpu.CompilerParams(vmem_limit_bytes=VMEM),
        cost_estimate=pl.CostEstimate(
            flops=2 * 18 * TILE * C * C + 10 * positions * TILE * C,
            bytes_accessed=18 * C * C * 2 + 8 * positions * C,
            transcendentals=0,
        ),
        name="back_rest",
    )(core, col, *frames, *weights, *conv_rest, *small, *large)


def shards(
    latent,
    grad_out,
    norm_gain,
    w_query,
    w_key,
    w_value,
    w_out,
    gain_one,
    gain_two,
    kernel_one,
    kernel_two,
):
    time_row = ("tm", "row")
    tm, row, col = lax.axis_index("tm"), lax.axis_index("row"), lax.axis_index("col")
    groups, cols = lax.axis_size("tm"), lax.axis_size("col")
    frames = groups * 2
    core = lax.rem(tm, 2)
    core_arg, col_arg = core.reshape(1), col.reshape(1)
    inverse_root = 1.0 / math.sqrt(C)
    swap_core = [(i, i ^ 1) for i in range(groups)]
    swap_row = [(0, 1), (1, 0)]

    def moved(value, steps):
        pairs = [(s, s + steps) for s in range(frames) if 0 <= s + steps < frames]
        return lax.ppermute(value, time_row, pairs)

    mine = lax.all_gather(
        jnp.where(core == 0, kernel_one, kernel_two), "col", axis=3, tiled=True
    ).reshape(27, C, C)

    keep = lax.dynamic_index_in_dim(latent, row, 0, keepdims=False)
    give = lax.dynamic_index_in_dim(latent, 1 - row, 0, keepdims=False)
    got = lax.ppermute(give, "row", swap_row)
    tile = jnp.concatenate([jnp.where(row == 0, keep, got), jnp.where(row == 0, got, keep)], axis=0)
    side = 4
    along_x = [[side * y + x for x in range(side)] for y in range(side)]
    along_y = [[side * y + x for y in range(side)] for x in range(side)]

    def shared(value, members):
        spread = jnp.broadcast_to(value[None], (side,) + value.shape)
        return lax.all_to_all(spread, "col", 0, 0, tiled=True, axis_index_groups=members)

    frame = shared(shared(tile.reshape(TILE, C), along_x), along_y)
    tiles = frame.reshape(cols, 2, 8, 8, C)
    pick = lambda index: lax.dynamic_index_in_dim(tiles, index, 0, keepdims=False)
    before, own, after = (
        pick(jnp.maximum(col - 1, 0)),
        pick(col),
        pick(jnp.minimum(col + 1, cols - 1)),
    )
    empty = jnp.zeros((2, 8, 4, C), BF16)
    window = jnp.concatenate([before[:, :, 6:], own, after[:, :, :2], empty], axis=2)
    window = window.reshape(SPAN, C)
    slot = lax.rem(lax.broadcasted_iota(jnp.int32, (SPAN, 1), 0), SLOTS)
    column = col * 8 + slot - 2
    inside = (column >= 0) & (column < cols * 8)
    wide_frame = frame.reshape(-1, C).astype(F32)
    normed = (wide_frame * norm_factor(wide_frame) * norm_gain).astype(BF16)
    keys = jnp.dot(normed, w_key, preferred_element_type=F32).astype(BF16)
    values = jnp.dot(normed, w_value, preferred_element_type=F32).astype(BF16)
    wide_window = window.astype(F32)
    normed_window = (wide_window * norm_factor(wide_window) * norm_gain).astype(BF16)
    queries = jnp.dot(normed_window, w_query, preferred_element_type=F32).astype(BF16)
    scores = jnp.einsum("kd,qd->kq", keys, queries, preferred_element_type=F32) * inverse_root
    prob = jax.nn.softmax(scores, axis=0)
    context = jnp.einsum(
        "kq,kd->qd", prob.astype(BF16), values, preferred_element_type=F32
    ).astype(BF16)
    mixed = (wide_window + jnp.dot(context, w_out, preferred_element_type=F32)).astype(BF16)
    wide_mixed = mixed.astype(F32)
    act_one = jax.nn.silu(wide_mixed * norm_factor(wide_mixed) * gain_one)
    act_one = jnp.where(inside & (slot < 12), act_one, 0.0).astype(BF16)

    def own_columns(value):
        return value.reshape(ROWS, SLOTS, C)[:, 2:10].reshape(TILE, C)

    own_queries = own_columns(queries)
    own_scores = jnp.einsum("kd,qd->kq", keys, own_queries, preferred_element_type=F32)
    own_prob = jax.nn.softmax(own_scores * inverse_root, axis=0)
    query_key = lax.dot_general(own_queries, w_key, NT, preferred_element_type=F32).astype(BF16)

    def framed(f0, f1, f2):
        stacked = jnp.stack([f.reshape(ROWS, SLOTS, C) for f in (f0, f1, f2)])
        return jnp.pad(stacked, ((0, 0), (1, 1), (0, 0), (0, 0)))

    act_frames = framed(moved(act_one, 2), moved(act_one, 1), act_one)

    keep = lax.dynamic_index_in_dim(grad_out, row, 0, keepdims=False)
    give = lax.dynamic_index_in_dim(grad_out, 1 - row, 0, keepdims=False)
    got = lax.ppermute(give, "row", swap_row)
    tile = jnp.concatenate([jnp.where(row == 0, keep, got), jnp.where(row == 0, got, keep)], axis=0)
    to_right = [(i, i + 1) for i in range(cols - 1)]
    to_left = [(i + 1, i) for i in range(cols - 1)]
    grad = jnp.concatenate(
        [
            lax.ppermute(tile[:, 6:], "col", to_right),
            tile,
            lax.ppermute(tile[:, :2], "col", to_left),
            jnp.zeros((ROWS, 4, C), BF16),
        ],
        axis=1,
    ).reshape(SPAN, C)
    grad_frames = framed(grad, moved(grad, -1), moved(grad, -2))

    ours = jnp.where(core == 0, act_frames, grad_frames)
    theirs = lax.ppermute(jnp.where(core == 0, grad_frames, act_frames), "tm", swap_core)
    both = jnp.stack([ours, theirs], axis=2).reshape(3, (ROWS + 2) * 2 * SLOTS, C)
    both, mine, own_prob, query_key = lax.optimization_barrier((both, mine, own_prob, query_key))
    other = lax.ppermute(mine, "tm", swap_core)
    sums = pair_conv(core_arg, both, mine).reshape(ROWS, 2, SLOTS, C)
    kept = sums[:, 0].reshape(SPAN, C)
    given = lax.ppermute(sums[:, 1].reshape(SPAN, C).astype(BF16), "tm", swap_core)
    conv_one = jnp.where(core == 0, kept.astype(BF16), given)
    g_act_two = jnp.where(core == 0, given.astype(F32), kept)
    wide_conv = conv_one.astype(F32)
    pre_two = wide_conv * norm_factor(wide_conv) * gain_two
    g_conv = norm_backward(wide_conv, gain_two, g_act_two * silu_slope(pre_two))
    g_conv = jnp.where(inside, g_conv, 0.0).astype(BF16)
    g_conv = g_conv.reshape(ROWS, SLOTS, C)[:, 1:11].reshape(ROWS * 10, C)
    later = [moved(g_conv, -2), moved(g_conv, -1)]
    own_part = back_own(core_arg, g_conv, mine, other)
    g_mixed, partial = back_rest(
        core_arg,
        col_arg,
        later,
        (mine, other),
        (own_part, own_columns(grad), own_columns(mixed), gain_one.reshape(1, C)),
        (query_key, w_out, w_value, w_query),
        (own_prob, keys, values),
    )

    halves = g_mixed.reshape(2, 8, 8, C)
    stay = lax.dynamic_index_in_dim(halves, row, 0, keepdims=False)
    leave = lax.dynamic_index_in_dim(halves, 1 - row, 0, keepdims=False)
    come = lax.ppermute(leave, "row", swap_row)
    g_tile = jnp.stack([jnp.where(row == 0, stay, come), jnp.where(row == 0, come, stay)])
    parts = lax.all_to_all(partial.reshape(-1, 64, C), ("row", "col"), 0, 0, tiled=True)
    g_normed = jnp.sum(parts.reshape(2, cols, 64, C).astype(F32), axis=1).reshape(latent.shape)

    wide_latent = latent.astype(F32)
    return g_tile.astype(F32) + norm_backward(wide_latent, norm_gain, g_normed)


def solution(mesh):
    placed = (
        P("tm", "row", "col", None),
        P("tm", "row", "col", None),
        P(),
        P(),
        P(),
        P(),
        P(),
        P(),
        P(),
        P(None, None, None, "col", None),
        P(None, None, None, "col", None),
    )
    return jax.shard_map(
        shards, mesh=mesh, in_specs=placed, out_specs=P("tm", "row", "col", None), check_vma=False
    )
```

```python
import math

import jax
import jax.numpy as jnp
from jax import lax
from jax.experimental import pallas as pl
from jax.experimental.pallas import tpu as pltpu
from jax.sharding import PartitionSpec as P

EPSILON = 1e-06
F32, BF16 = jnp.float32, jnp.bfloat16
C = 384
ROWS, SLOTS = 16, 16
SPAN = ROWS * SLOTS
TILE = ROWS * 8
VMEM = 50 * 1024 * 1024
NT = (((1,), (1,)), ((), ()))


def norm_factor(field):
    return lax.rsqrt(jnp.mean(field * field, axis=-1, keepdims=True) + EPSILON)


def norm_backward(field, gain, upstream):
    factor = norm_factor(field)
    gained = gain * upstream
    return factor * gained - field * factor**3 * jnp.mean(field * gained, axis=-1, keepdims=True)


def silu_slope(pre):
    sig = jax.nn.sigmoid(pre)
    return sig * (1.0 + pre * (1.0 - sig))


def stage_shifts(x_ref, s_ref):
    length = x_ref.shape[1]
    for frame in range(3):
        wide = x_ref[frame].astype(F32)
        s_ref[frame, :, :C] = pltpu.roll(wide, 1, 0).astype(BF16)
        s_ref[frame, :, C : 2 * C] = x_ref[frame]
        s_ref[frame, :, 2 * C :] = pltpu.roll(wide, length - 1, 0).astype(BF16)


def fetch(core, mine_ref, other_ref, w_ref, sem, begin):
    count = w_ref.shape[0] // 3

    def copy(source, triple):
        return pltpu.make_async_copy(
            source.at[pl.ds(3 * (begin + triple), 3)], w_ref.at[pl.ds(3 * triple, 3)], sem.at[triple]
        )

    for triple in range(count):
        if other_ref is None:
            copy(mine_ref, triple).start()
        else:
            pl.when(core == 0)(lambda triple=triple: copy(mine_ref, triple).start())
            pl.when(core != 0)(lambda triple=triple: copy(other_ref, triple).start())
    return lambda triple: copy(mine_ref, triple).wait()


def pair_kernel(core_ref, x_ref, mine_ref, out_ref, s_ref, w_ref, sem):
    pitch, span = 2 * SLOTS, 2 * SPAN
    arrived = fetch(None, mine_ref, None, w_ref, sem, 0)
    stage_shifts(x_ref, s_ref)

    def windows(depth, down, lanes):
        return s_ref[depth, down * pitch : down * pitch + span, lanes]

    for group in ((0,), (1, 2), (3, 4, 5), (6, 7, 8)):
        for triple in group:
            arrived(triple)
        depth, first = group[0] // 3, group[0] == 0
        downs = [triple % 3 for triple in group]
        taps = range(3 * group[0], 3 * group[-1] + 3)

        def add(term, first=first):
            out_ref[...] = term if first else out_ref[...] + term

        @pl.when(core_ref[0] == 0)
        def _():
            window = jnp.concatenate(
                [windows(depth, down, slice(0, 3 * C)) for down in downs], axis=1
            )
            matrix = w_ref[taps[0] : taps[-1] + 1].reshape(len(taps) * C, C)
            add(jnp.dot(window, matrix, preferred_element_type=F32))

        @pl.when(core_ref[0] != 0)
        def _():
            window = jnp.concatenate(
                [
                    windows(2 - depth, 2 - down, slice((2 - across) * C, (3 - across) * C))
                    for down in downs
                    for across in range(3)
                ],
                axis=1,
            )
            matrix = jnp.concatenate([w_ref[tap] for tap in taps], axis=1)
            add(lax.dot_general(window, matrix, NT, preferred_element_type=F32))


def pair_conv(core, x, mine):
    vmem = pl.BlockSpec(memory_space=pltpu.VMEM)
    return pl.pallas_call(
        pair_kernel,
        out_shape=jax.ShapeDtypeStruct((2 * SPAN, C), F32),
        in_specs=[pl.BlockSpec(memory_space=pltpu.SMEM), vmem, pl.BlockSpec(memory_space=pl.ANY)],
        out_specs=vmem,
        scratch_shapes=[
            pltpu.VMEM((3, x.shape[1], 3 * C), BF16),
            pltpu.VMEM((27, C, C), BF16),
            pltpu.SemaphoreType.DMA((9,)),
        ],
        compiler_params=pltpu.CompilerParams(vmem_limit_bytes=VMEM),
        cost_estimate=pl.CostEstimate(
            flops=2 * 27 * 2 * SPAN * C * C, bytes_accessed=27 * C * C * 2, transcendentals=0
        ),
        name="pair_conv",
    )(core, x, mine)


def window_of(frame_ref, place, s_ref, wide_ref, tile_ref):
    wide_ref[...] = frame_ref[...].astype(F32)
    for shift in range(3):
        for r in range(ROWS):
            tile_ref[shift, 8 + r * 8 : 16 + r * 8, :] = wide_ref[
                r * 10 + shift : r * 10 + shift + 8, :
            ]
        for down in range(3):
            s_ref[place, down, :, shift * C : (shift + 1) * C] = tile_ref[
                shift, down * 8 : down * 8 + TILE, :
            ].astype(BF16)


def back_taps(frame_refs, arrived, s_ref, wide_ref, tile_ref, w_ref, total):
    tile_ref[:, :8, :] = jnp.zeros((3, 8, C), F32)
    tile_ref[:, 8 + TILE :, :] = jnp.zeros((3, 8, C), F32)
    for place, frame_ref in enumerate(frame_refs):
        window_of(frame_ref, place, s_ref, wide_ref, tile_ref)
    for triple in range(3 * len(frame_refs)):
        arrived(triple)
        place, down = triple // 3, triple % 3
        for across in range(3):
            lane = (2 - across) * C
            window = s_ref[place, 2 - down, :, lane : lane + C]
            total += lax.dot_general(
                window, w_ref[3 * triple + across], NT, preferred_element_type=F32
            )
    return total


def own_kernel(core_ref, frame_ref, mine_ref, other_ref, out_ref, s_ref, wide_ref, tile_ref, w_ref, sem):
    arrived = fetch(core_ref[0], mine_ref, other_ref, w_ref, sem, 6)
    zero = jnp.zeros((TILE, C), F32)
    out_ref[...] = back_taps([frame_ref], arrived, s_ref, wide_ref, tile_ref, w_ref, zero)


def back_scratch(count):
    return [
        pltpu.VMEM((count, 3, TILE, 3 * C), BF16),
        pltpu.VMEM((ROWS * 10, C), F32),
        pltpu.VMEM((3, TILE + 16, C), F32),
        pltpu.VMEM((9 * count, C, C), BF16),
        pltpu.SemaphoreType.DMA((3 * count,)),
    ]


def back_own(core, frame, mine, other):
    smem, vmem = pl.BlockSpec(memory_space=pltpu.SMEM), pl.BlockSpec(memory_space=pltpu.VMEM)
    remain = pl.BlockSpec(memory_space=pl.ANY)
    return pl.pallas_call(
        own_kernel,
        out_shape=jax.ShapeDtypeStruct((TILE, C), F32),
        in_specs=[smem, vmem, remain, remain],
        out_specs=vmem,
        scratch_shapes=back_scratch(1),
        compiler_params=pltpu.CompilerParams(vmem_limit_bytes=VMEM),
        cost_estimate=pl.CostEstimate(
            flops=2 * 9 * TILE * C * C, bytes_accessed=9 * C * C * 2, transcendentals=0
        ),
        name="back_own",
    )(core, frame, mine, other)


CHUNK = 2048


def back_kernel(
    core_ref, col_ref, late_ref, soon_ref, mine_ref, other_ref, start_ref, grad_ref, mixed_ref, gain_ref,
    qk_ref, w_out_ref, w_value_ref, w_query_ref, prob_from, keys_from, values_from,
    gm_ref, out_ref,
    s_ref, wide_ref, tile_ref, w_ref, sem, prob_ref, keys_ref, values_ref, in_sem,
    gp_ref, mix_ref, right_ref,
):
    arrived = fetch(core_ref[0], mine_ref, other_ref, w_ref, sem, 0)
    pairs = ((values_from, values_ref), (prob_from, prob_ref), (keys_from, keys_ref))
    inputs = [
        pltpu.make_async_copy(source, target, in_sem.at[i])
        for i, (source, target) in enumerate(pairs)
    ]
    for copy in inputs:
        copy.start()
    total = back_taps(
        [late_ref, soon_ref], arrived, s_ref, wide_ref, tile_ref, w_ref, start_ref[...]
    )
    mixed = mixed_ref[...].astype(F32)
    gain = gain_ref[...]
    slope = silu_slope(mixed * norm_factor(mixed) * gain)
    total = grad_ref[...].astype(F32) + norm_backward(mixed, gain, total * slope)
    g_mixed = total.astype(BF16)
    gm_ref[...] = g_mixed

    positions = keys_ref.shape[0]
    count = positions // CHUNK
    inverse_root = 1.0 / math.sqrt(C)
    g_context = lax.dot_general(g_mixed, w_out_ref[...], NT, preferred_element_type=F32)
    g_context = g_context.astype(BF16)
    right_ref[:TILE, :] = qk_ref[...]
    right_ref[TILE:, :] = lax.dot_general(
        g_context, w_value_ref[...], NT, preferred_element_type=F32
    ).astype(BF16)
    for copy in inputs:
        copy.wait()
    delta = jnp.zeros((1, TILE), F32)
    for c in range(count):
        part = pl.ds(c * CHUNK, CHUNK)
        g_prob = lax.dot_general(values_ref[part, :], g_context, NT, preferred_element_type=F32)
        gp_ref[part, :] = g_prob
        delta = delta + jnp.sum(prob_ref[part, :] * g_prob, axis=0, keepdims=True)
    g_query = jnp.zeros((TILE, C), F32)
    for c in range(count):
        part = pl.ds(c * CHUNK, CHUNK)
        prob = prob_ref[part, :]
        g_score = (prob * (gp_ref[part, :] - delta) * inverse_root).astype(BF16)
        mix_ref[:, :TILE] = g_score
        mix_ref[:, TILE:] = prob.astype(BF16)
        sums = jnp.dot(mix_ref[...], right_ref[...], preferred_element_type=F32).astype(BF16)
        for piece in range(CHUNK // 64):
            tile, half = c * CHUNK // TILE + piece // 2, piece % 2
            there = half * (positions // 2) + tile * 64
            out_ref[there : there + 64, :] = sums[piece * 64 : piece * 64 + 64]
        g_query += lax.dot_general(
            g_score, keys_ref[part, :], (((0,), (0,)), ((), ())), preferred_element_type=F32
        )
    high = g_query.astype(BF16)
    low = (g_query - high.astype(F32)).astype(BF16)
    local = lax.dot_general(high, w_query_ref[...], NT, preferred_element_type=F32)
    local += lax.dot_general(low, w_query_ref[...], NT, preferred_element_type=F32)
    own = pl.ds(pl.multiple_of(col_ref[0] * TILE, TILE), TILE)
    prob = prob_ref[own, :]
    mix_ref[:TILE, :TILE] = (prob * (gp_ref[own, :] - delta) * inverse_root).astype(BF16)
    mix_ref[:TILE, TILE:] = prob.astype(BF16)
    local += jnp.dot(mix_ref[:TILE, :], right_ref[...], preferred_element_type=F32)
    for half in range(2):
        there = pl.multiple_of(half * (positions // 2) + col_ref[0] * 64, 64)
        out_ref[pl.ds(there, 64), :] = local[half * 64 : half * 64 + 64].astype(BF16)


def back_rest(core, col, frames, weights, conv_rest, small, large):
    positions = large[1].shape[0]
    smem, vmem = pl.BlockSpec(memory_space=pltpu.SMEM), pl.BlockSpec(memory_space=pltpu.VMEM)
    remain = pl.BlockSpec(memory_space=pl.ANY)
    return pl.pallas_call(
        back_kernel,
        out_shape=(
            jax.ShapeDtypeStruct((TILE, C), BF16),
            jax.ShapeDtypeStruct((positions, C), BF16),
        ),
        in_specs=[smem] * 2 + [vmem] * 2 + [remain] * 2 + [vmem] * 8 + [remain] * 3,
        out_specs=(vmem, vmem),
        scratch_shapes=back_scratch(2)
        + [
            pltpu.VMEM((positions, TILE), F32),
            pltpu.VMEM((positions, C), BF16),
            pltpu.VMEM((positions, C), BF16),
            pltpu.SemaphoreType.DMA((3,)),
            pltpu.VMEM((positions, TILE), F32),
            pltpu.VMEM((CHUNK, 2 * TILE), BF16),
            pltpu.VMEM((2 * TILE, C), BF16),
        ],
        compiler_params=pltpu.CompilerParams(vmem_limit_bytes=VMEM),
        cost_estimate=pl.CostEstimate(
            flops=2 * 18 * TILE * C * C + 10 * positions * TILE * C,
            bytes_accessed=18 * C * C * 2 + 8 * positions * C,
            transcendentals=0,
        ),
        name="back_rest",
    )(core, col, *frames, *weights, *conv_rest, *small, *large)


def shards(
    latent,
    grad_out,
    norm_gain,
    w_query,
    w_key,
    w_value,
    w_out,
    gain_one,
    gain_two,
    kernel_one,
    kernel_two,
):
    time_row = ("tm", "row")
    tm, row, col = lax.axis_index("tm"), lax.axis_index("row"), lax.axis_index("col")
    groups, cols = lax.axis_size("tm"), lax.axis_size("col")
    frames = groups * 2
    core = lax.rem(tm, 2)
    core_arg, col_arg = core.reshape(1), col.reshape(1)
    inverse_root = 1.0 / math.sqrt(C)
    swap_core = [(i, i ^ 1) for i in range(groups)]
    swap_row = [(0, 1), (1, 0)]

    def moved(value, steps):
        pairs = [(s, s + steps) for s in range(frames) if 0 <= s + steps < frames]
        return lax.ppermute(value, time_row, pairs)

    mine = lax.all_gather(
        jnp.where(core == 0, kernel_one, kernel_two), "col", axis=3, tiled=True
    ).reshape(27, C, C)

    keep = lax.dynamic_index_in_dim(latent, row, 0, keepdims=False)
    give = lax.dynamic_index_in_dim(latent, 1 - row, 0, keepdims=False)
    got = lax.ppermute(give, "row", swap_row)
    tile = jnp.concatenate([jnp.where(row == 0, keep, got), jnp.where(row == 0, got, keep)], axis=0)
    side = 4
    along_x = [[side * y + x for x in range(side)] for y in range(side)]
    along_y = [[side * y + x for y in range(side)] for x in range(side)]

    def shared(value, members):
        spread = jnp.broadcast_to(value[None], (side,) + value.shape)
        return lax.all_to_all(spread, "col", 0, 0, tiled=True, axis_index_groups=members)

    frame = shared(shared(tile.reshape(TILE, C), along_x), along_y)
    tiles = frame.reshape(cols, 2, 8, 8, C)
    pick = lambda index: lax.dynamic_index_in_dim(tiles, index, 0, keepdims=False)
    before, own, after = (
        pick(jnp.maximum(col - 1, 0)),
        pick(col),
        pick(jnp.minimum(col + 1, cols - 1)),
    )
    empty = jnp.zeros((2, 8, 4, C), BF16)
    window = jnp.concatenate([before[:, :, 6:], own, after[:, :, :2], empty], axis=2)
    window = window.reshape(SPAN, C)
    slot = lax.rem(lax.broadcasted_iota(jnp.int32, (SPAN, 1), 0), SLOTS)
    column = col * 8 + slot - 2
    inside = (column >= 0) & (column < cols * 8)
    wide_frame = frame.reshape(-1, C).astype(F32)
    normed = (wide_frame * norm_factor(wide_frame) * norm_gain).astype(BF16)
    keys = jnp.dot(normed, w_key, preferred_element_type=F32).astype(BF16)
    values = jnp.dot(normed, w_value, preferred_element_type=F32).astype(BF16)
    wide_window = window.astype(F32)
    normed_window = (wide_window * norm_factor(wide_window) * norm_gain).astype(BF16)
    queries = jnp.dot(normed_window, w_query, preferred_element_type=F32).astype(BF16)
    scores = jnp.einsum("kd,qd->kq", keys, queries, preferred_element_type=F32) * inverse_root
    prob = jax.nn.softmax(scores, axis=0)
    context = jnp.einsum(
        "kq,kd->qd", prob.astype(BF16), values, preferred_element_type=F32
    ).astype(BF16)
    mixed = (wide_window + jnp.dot(context, w_out, preferred_element_type=F32)).astype(BF16)
    wide_mixed = mixed.astype(F32)
    act_one = jax.nn.silu(wide_mixed * norm_factor(wide_mixed) * gain_one)
    act_one = jnp.where(inside & (slot < 12), act_one, 0.0).astype(BF16)

    def own_columns(value):
        return value.reshape(ROWS, SLOTS, C)[:, 2:10].reshape(TILE, C)

    own_queries = own_columns(queries)
    own_scores = jnp.einsum("kd,qd->kq", keys, own_queries, preferred_element_type=F32)
    own_prob = jax.nn.softmax(own_scores * inverse_root, axis=0)
    query_key = lax.dot_general(own_queries, w_key, NT, preferred_element_type=F32).astype(BF16)

    def framed(f0, f1, f2):
        stacked = jnp.stack([f.reshape(ROWS, SLOTS, C) for f in (f0, f1, f2)])
        return jnp.pad(stacked, ((0, 0), (1, 1), (0, 0), (0, 0)))

    act_frames = framed(moved(act_one, 2), moved(act_one, 1), act_one)

    keep = lax.dynamic_index_in_dim(grad_out, row, 0, keepdims=False)
    give = lax.dynamic_index_in_dim(grad_out, 1 - row, 0, keepdims=False)
    got = lax.ppermute(give, "row", swap_row)
    tile = jnp.concatenate([jnp.where(row == 0, keep, got), jnp.where(row == 0, got, keep)], axis=0)
    to_right = [(i, i + 1) for i in range(cols - 1)]
    to_left = [(i + 1, i) for i in range(cols - 1)]
    grad = jnp.concatenate(
        [
            lax.ppermute(tile[:, 6:], "col", to_right),
            tile,
            lax.ppermute(tile[:, :2], "col", to_left),
            jnp.zeros((ROWS, 4, C), BF16),
        ],
        axis=1,
    ).reshape(SPAN, C)
    grad_frames = framed(grad, moved(grad, -1), moved(grad, -2))

    ours = jnp.where(core == 0, act_frames, grad_frames)
    theirs = lax.ppermute(jnp.where(core == 0, grad_frames, act_frames), "tm", swap_core)
    both = jnp.stack([ours, theirs], axis=2).reshape(3, (ROWS + 2) * 2 * SLOTS, C)
    both, mine, own_prob, query_key = lax.optimization_barrier((both, mine, own_prob, query_key))
    other = lax.ppermute(mine, "tm", swap_core)
    sums = pair_conv(core_arg, both, mine).reshape(ROWS, 2, SLOTS, C)
    kept = sums[:, 0].reshape(SPAN, C)
    given = lax.ppermute(sums[:, 1].reshape(SPAN, C).astype(BF16), "tm", swap_core)
    conv_one = jnp.where(core == 0, kept.astype(BF16), given)
    g_act_two = jnp.where(core == 0, given.astype(F32), kept)
    wide_conv = conv_one.astype(F32)
    pre_two = wide_conv * norm_factor(wide_conv) * gain_two
    g_conv = norm_backward(wide_conv, gain_two, g_act_two * silu_slope(pre_two))
    g_conv = jnp.where(inside, g_conv, 0.0).astype(BF16)
    g_conv = g_conv.reshape(ROWS, SLOTS, C)[:, 1:11].reshape(ROWS * 10, C)
    later = [moved(g_conv, -2), moved(g_conv, -1)]
    own_part = back_own(core_arg, g_conv, mine, other)
    g_mixed, partial = back_rest(
        core_arg,
        col_arg,
        later,
        (mine, other),
        (own_part, own_columns(grad), own_columns(mixed), gain_one.reshape(1, C)),
        (query_key, w_out, w_value, w_query),
        (own_prob, keys, values),
    )

    halves = g_mixed.reshape(2, 8, 8, C)
    stay = lax.dynamic_index_in_dim(halves, row, 0, keepdims=False)
    leave = lax.dynamic_index_in_dim(halves, 1 - row, 0, keepdims=False)
    come = lax.ppermute(leave, "row", swap_row)
    g_tile = jnp.stack([jnp.where(row == 0, stay, come), jnp.where(row == 0, come, stay)])
    parts = lax.all_to_all(partial.reshape(-1, 64, C), ("row", "col"), 0, 0, tiled=True)
    g_normed = jnp.sum(parts.reshape(2, cols, 64, C).astype(F32), axis=1).reshape(latent.shape)

    wide_latent = latent.astype(F32)
    return g_tile.astype(F32) + norm_backward(wide_latent, norm_gain, g_normed)


def solution(mesh):
    placed = (
        P("tm", "row", "col", None),
        P("tm", "row", "col", None),
        P(),
        P(),
        P(),
        P(),
        P(),
        P(),
        P(),
        P(None, None, None, "col", None),
        P(None, None, None, "col", None),
    )
    return jax.shard_map(
        shards, mesh=mesh, in_specs=placed, out_specs=P("tm", "row", "col", None), check_vma=False
    )
```

```python
import math

import jax
import jax.numpy as jnp
from jax import lax
from jax.experimental import pallas as pl
from jax.experimental.pallas import tpu as pltpu
from jax.sharding import PartitionSpec as P

EPSILON = 1e-06
F32, BF16 = jnp.float32, jnp.bfloat16
C = 384
ROWS, SLOTS = 16, 16
SPAN = ROWS * SLOTS
TILE = ROWS * 8
VMEM = 50 * 1024 * 1024
NT = (((1,), (1,)), ((), ()))


def norm_factor(field):
    return lax.rsqrt(jnp.mean(field * field, axis=-1, keepdims=True) + EPSILON)


def norm_backward(field, gain, upstream):
    factor = norm_factor(field)
    gained = gain * upstream
    return factor * gained - field * factor**3 * jnp.mean(field * gained, axis=-1, keepdims=True)


def silu_slope(pre):
    sig = jax.nn.sigmoid(pre)
    return sig * (1.0 + pre * (1.0 - sig))


def stage_shifts(x_ref, s_ref):
    length = x_ref.shape[1]
    for frame in range(3):
        wide = x_ref[frame].astype(F32)
        s_ref[frame, :, :C] = pltpu.roll(wide, 1, 0).astype(BF16)
        s_ref[frame, :, C : 2 * C] = x_ref[frame]
        s_ref[frame, :, 2 * C :] = pltpu.roll(wide, length - 1, 0).astype(BF16)


def fetch(core, mine_ref, other_ref, w_ref, sem, begin):
    count = w_ref.shape[0] // 3

    def copy(source, triple):
        return pltpu.make_async_copy(
            source.at[pl.ds(3 * (begin + triple), 3)], w_ref.at[pl.ds(3 * triple, 3)], sem.at[triple]
        )

    for triple in range(count):
        if other_ref is None:
            copy(mine_ref, triple).start()
        else:
            pl.when(core == 0)(lambda triple=triple: copy(mine_ref, triple).start())
            pl.when(core != 0)(lambda triple=triple: copy(other_ref, triple).start())
    return lambda triple: copy(mine_ref, triple).wait()


def pair_kernel(core_ref, x_ref, mine_ref, out_ref, s_ref, w_ref, sem):
    pitch, span = 2 * SLOTS, 2 * SPAN
    arrived = fetch(None, mine_ref, None, w_ref, sem, 0)
    stage_shifts(x_ref, s_ref)

    def windows(depth, down, lanes):
        return s_ref[depth, down * pitch : down * pitch + span, lanes]

    for group in ((0,), (1, 2), (3, 4, 5), (6, 7, 8)):
        for triple in group:
            arrived(triple)
        depth, first = group[0] // 3, group[0] == 0
        downs = [triple % 3 for triple in group]
        taps = range(3 * group[0], 3 * group[-1] + 3)

        def add(term, first=first):
            out_ref[...] = term if first else out_ref[...] + term

        @pl.when(core_ref[0] == 0)
        def _():
            window = jnp.concatenate(
                [windows(depth, down, slice(0, 3 * C)) for down in downs], axis=1
            )
            matrix = w_ref[taps[0] : taps[-1] + 1].reshape(len(taps) * C, C)
            add(jnp.dot(window, matrix, preferred_element_type=F32))

        @pl.when(core_ref[0] != 0)
        def _():
            window = jnp.concatenate(
                [
                    windows(2 - depth, 2 - down, slice((2 - across) * C, (3 - across) * C))
                    for down in downs
                    for across in range(3)
                ],
                axis=1,
            )
            matrix = jnp.concatenate([w_ref[tap] for tap in taps], axis=1)
            add(lax.dot_general(window, matrix, NT, preferred_element_type=F32))


def pair_conv(core, x, mine):
    vmem = pl.BlockSpec(memory_space=pltpu.VMEM)
    return pl.pallas_call(
        pair_kernel,
        out_shape=jax.ShapeDtypeStruct((2 * SPAN, C), F32),
        in_specs=[pl.BlockSpec(memory_space=pltpu.SMEM), vmem, pl.BlockSpec(memory_space=pl.ANY)],
        out_specs=vmem,
        scratch_shapes=[
            pltpu.VMEM((3, x.shape[1], 3 * C), BF16),
            pltpu.VMEM((27, C, C), BF16),
            pltpu.SemaphoreType.DMA((9,)),
        ],
        compiler_params=pltpu.CompilerParams(vmem_limit_bytes=VMEM),
        cost_estimate=pl.CostEstimate(
            flops=2 * 27 * 2 * SPAN * C * C, bytes_accessed=27 * C * C * 2, transcendentals=0
        ),
        name="pair_conv",
    )(core, x, mine)


def window_of(frame_ref, place, s_ref, wide_ref, tile_ref):
    wide_ref[...] = frame_ref[...].astype(F32)
    for shift in range(3):
        for r in range(ROWS):
            tile_ref[shift, 8 + r * 8 : 16 + r * 8, :] = wide_ref[
                r * 10 + shift : r * 10 + shift + 8, :
            ]
        for down in range(3):
            s_ref[place, down, :, shift * C : (shift + 1) * C] = tile_ref[
                shift, down * 8 : down * 8 + TILE, :
            ].astype(BF16)


def back_taps(frame_refs, arrived, s_ref, wide_ref, tile_ref, w_ref, total):
    tile_ref[:, :8, :] = jnp.zeros((3, 8, C), F32)
    tile_ref[:, 8 + TILE :, :] = jnp.zeros((3, 8, C), F32)
    for place, frame_ref in enumerate(frame_refs):
        window_of(frame_ref, place, s_ref, wide_ref, tile_ref)
    for triple in range(3 * len(frame_refs)):
        arrived(triple)
        place, down = triple // 3, triple % 3
        for across in range(3):
            lane = (2 - across) * C
            window = s_ref[place, 2 - down, :, lane : lane + C]
            total += lax.dot_general(
                window, w_ref[3 * triple + across], NT, preferred_element_type=F32
            )
    return total


def own_kernel(core_ref, frame_ref, mine_ref, other_ref, out_ref, s_ref, wide_ref, tile_ref, w_ref, sem):
    arrived = fetch(core_ref[0], mine_ref, other_ref, w_ref, sem, 6)
    zero = jnp.zeros((TILE, C), F32)
    out_ref[...] = back_taps([frame_ref], arrived, s_ref, wide_ref, tile_ref, w_ref, zero)


def back_scratch(count):
    return [
        pltpu.VMEM((count, 3, TILE, 3 * C), BF16),
        pltpu.VMEM((ROWS * 10, C), F32),
        pltpu.VMEM((3, TILE + 16, C), F32),
        pltpu.VMEM((9 * count, C, C), BF16),
        pltpu.SemaphoreType.DMA((3 * count,)),
    ]


def back_own(core, frame, mine, other):
    smem, vmem = pl.BlockSpec(memory_space=pltpu.SMEM), pl.BlockSpec(memory_space=pltpu.VMEM)
    remain = pl.BlockSpec(memory_space=pl.ANY)
    return pl.pallas_call(
        own_kernel,
        out_shape=jax.ShapeDtypeStruct((TILE, C), F32),
        in_specs=[smem, vmem, remain, remain],
        out_specs=vmem,
        scratch_shapes=back_scratch(1),
        compiler_params=pltpu.CompilerParams(vmem_limit_bytes=VMEM),
        cost_estimate=pl.CostEstimate(
            flops=2 * 9 * TILE * C * C, bytes_accessed=9 * C * C * 2, transcendentals=0
        ),
        name="back_own",
    )(core, frame, mine, other)


CHUNK = 2048


def back_kernel(
    core_ref, col_ref, late_ref, soon_ref, mine_ref, other_ref, start_ref, grad_ref, mixed_ref, gain_ref,
    qk_ref, w_out_ref, w_value_ref, w_query_ref, prob_from, keys_from, values_from,
    gm_ref, out_ref,
    s_ref, wide_ref, tile_ref, w_ref, sem, prob_ref, keys_ref, values_ref, in_sem,
    gp_ref, mix_ref, right_ref,
):
    arrived = fetch(core_ref[0], mine_ref, other_ref, w_ref, sem, 0)
    pairs = ((values_from, values_ref), (prob_from, prob_ref), (keys_from, keys_ref))
    inputs = [
        pltpu.make_async_copy(source, target, in_sem.at[i])
        for i, (source, target) in enumerate(pairs)
    ]
    for copy in inputs:
        copy.start()
    total = back_taps(
        [late_ref, soon_ref], arrived, s_ref, wide_ref, tile_ref, w_ref, start_ref[...]
    )
    mixed = mixed_ref[...].astype(F32)
    gain = gain_ref[...]
    slope = silu_slope(mixed * norm_factor(mixed) * gain)
    total = grad_ref[...].astype(F32) + norm_backward(mixed, gain, total * slope)
    g_mixed = total.astype(BF16)
    gm_ref[...] = g_mixed

    positions = keys_ref.shape[0]
    count = positions // CHUNK
    inverse_root = 1.0 / math.sqrt(C)
    g_context = lax.dot_general(g_mixed, w_out_ref[...], NT, preferred_element_type=F32)
    g_context = g_context.astype(BF16)
    right_ref[:TILE, :] = qk_ref[...]
    right_ref[TILE:, :] = lax.dot_general(
        g_context, w_value_ref[...], NT, preferred_element_type=F32
    ).astype(BF16)
    inputs[0].wait()
    inputs[1].wait()
    delta = jnp.zeros((1, TILE), F32)
    for c in range(count):
        part = pl.ds(c * CHUNK, CHUNK)
        g_prob = lax.dot_general(values_ref[part, :], g_context, NT, preferred_element_type=F32)
        gp_ref[part, :] = g_prob
        delta = delta + jnp.sum(prob_ref[part, :] * g_prob, axis=0, keepdims=True)
    inputs[2].wait()
    g_query = jnp.zeros((TILE, C), F32)
    for c in range(count):
        part = pl.ds(c * CHUNK, CHUNK)
        prob = prob_ref[part, :]
        g_score = (prob * (gp_ref[part, :] - delta) * inverse_root).astype(BF16)
        mix_ref[:, :TILE] = g_score
        mix_ref[:, TILE:] = prob.astype(BF16)
        sums = jnp.dot(mix_ref[...], right_ref[...], preferred_element_type=F32).astype(BF16)
        for piece in range(CHUNK // 64):
            tile, half = c * CHUNK // TILE + piece // 2, piece % 2
            there = half * (positions // 2) + tile * 64
            out_ref[there : there + 64, :] = sums[piece * 64 : piece * 64 + 64]
        g_query += lax.dot_general(
            g_score, keys_ref[part, :], (((0,), (0,)), ((), ())), preferred_element_type=F32
        )
    high = g_query.astype(BF16)
    low = (g_query - high.astype(F32)).astype(BF16)
    local = lax.dot_general(high, w_query_ref[...], NT, preferred_element_type=F32)
    local += lax.dot_general(low, w_query_ref[...], NT, preferred_element_type=F32)
    own = pl.ds(pl.multiple_of(col_ref[0] * TILE, TILE), TILE)
    prob = prob_ref[own, :]
    mix_ref[:TILE, :TILE] = (prob * (gp_ref[own, :] - delta) * inverse_root).astype(BF16)
    mix_ref[:TILE, TILE:] = prob.astype(BF16)
    local += jnp.dot(mix_ref[:TILE, :], right_ref[...], preferred_element_type=F32)
    for half in range(2):
        there = pl.multiple_of(half * (positions // 2) + col_ref[0] * 64, 64)
        out_ref[pl.ds(there, 64), :] = local[half * 64 : half * 64 + 64].astype(BF16)


def back_rest(core, col, frames, weights, conv_rest, small, large):
    positions = large[1].shape[0]
    smem, vmem = pl.BlockSpec(memory_space=pltpu.SMEM), pl.BlockSpec(memory_space=pltpu.VMEM)
    remain = pl.BlockSpec(memory_space=pl.ANY)
    return pl.pallas_call(
        back_kernel,
        out_shape=(
            jax.ShapeDtypeStruct((TILE, C), BF16),
            jax.ShapeDtypeStruct((positions, C), BF16),
        ),
        in_specs=[smem] * 2 + [vmem] * 2 + [remain] * 2 + [vmem] * 8 + [remain] * 3,
        out_specs=(vmem, vmem),
        scratch_shapes=back_scratch(2)
        + [
            pltpu.VMEM((positions, TILE), F32),
            pltpu.VMEM((positions, C), BF16),
            pltpu.VMEM((positions, C), BF16),
            pltpu.SemaphoreType.DMA((3,)),
            pltpu.VMEM((positions, TILE), F32),
            pltpu.VMEM((CHUNK, 2 * TILE), BF16),
            pltpu.VMEM((2 * TILE, C), BF16),
        ],
        compiler_params=pltpu.CompilerParams(vmem_limit_bytes=VMEM),
        cost_estimate=pl.CostEstimate(
            flops=2 * 18 * TILE * C * C + 10 * positions * TILE * C,
            bytes_accessed=18 * C * C * 2 + 8 * positions * C,
            transcendentals=0,
        ),
        name="back_rest",
    )(core, col, *frames, *weights, *conv_rest, *small, *large)


def shards(
    latent,
    grad_out,
    norm_gain,
    w_query,
    w_key,
    w_value,
    w_out,
    gain_one,
    gain_two,
    kernel_one,
    kernel_two,
):
    time_row = ("tm", "row")
    tm, row, col = lax.axis_index("tm"), lax.axis_index("row"), lax.axis_index("col")
    groups, cols = lax.axis_size("tm"), lax.axis_size("col")
    frames = groups * 2
    core = lax.rem(tm, 2)
    core_arg, col_arg = core.reshape(1), col.reshape(1)
    inverse_root = 1.0 / math.sqrt(C)
    swap_core = [(i, i ^ 1) for i in range(groups)]
    swap_row = [(0, 1), (1, 0)]

    def moved(value, steps):
        pairs = [(s, s + steps) for s in range(frames) if 0 <= s + steps < frames]
        return lax.ppermute(value, time_row, pairs)

    mine = lax.all_gather(
        jnp.where(core == 0, kernel_one, kernel_two), "col", axis=3, tiled=True
    ).reshape(27, C, C)

    keep = lax.dynamic_index_in_dim(latent, row, 0, keepdims=False)
    give = lax.dynamic_index_in_dim(latent, 1 - row, 0, keepdims=False)
    got = lax.ppermute(give, "row", swap_row)
    tile = jnp.concatenate([jnp.where(row == 0, keep, got), jnp.where(row == 0, got, keep)], axis=0)
    side = 4
    along_x = [[side * y + x for x in range(side)] for y in range(side)]
    along_y = [[side * y + x for y in range(side)] for x in range(side)]

    def shared(value, members):
        spread = jnp.broadcast_to(value[None], (side,) + value.shape)
        return lax.all_to_all(spread, "col", 0, 0, tiled=True, axis_index_groups=members)

    frame = shared(shared(tile.reshape(TILE, C), along_x), along_y)
    tiles = frame.reshape(cols, 2, 8, 8, C)
    pick = lambda index: lax.dynamic_index_in_dim(tiles, index, 0, keepdims=False)
    before, own, after = (
        pick(jnp.maximum(col - 1, 0)),
        pick(col),
        pick(jnp.minimum(col + 1, cols - 1)),
    )
    empty = jnp.zeros((2, 8, 4, C), BF16)
    window = jnp.concatenate([before[:, :, 6:], own, after[:, :, :2], empty], axis=2)
    window = window.reshape(SPAN, C)
    slot = lax.rem(lax.broadcasted_iota(jnp.int32, (SPAN, 1), 0), SLOTS)
    column = col * 8 + slot - 2
    inside = (column >= 0) & (column < cols * 8)
    wide_frame = frame.reshape(-1, C).astype(F32)
    normed = (wide_frame * norm_factor(wide_frame) * norm_gain).astype(BF16)
    keys = jnp.dot(normed, w_key, preferred_element_type=F32).astype(BF16)
    values = jnp.dot(normed, w_value, preferred_element_type=F32).astype(BF16)
    wide_window = window.astype(F32)
    normed_window = (wide_window * norm_factor(wide_window) * norm_gain).astype(BF16)
    queries = jnp.dot(normed_window, w_query, preferred_element_type=F32).astype(BF16)
    scores = jnp.einsum("kd,qd->kq", keys, queries, preferred_element_type=F32) * inverse_root
    prob = jax.nn.softmax(scores, axis=0)
    context = jnp.einsum(
        "kq,kd->qd", prob.astype(BF16), values, preferred_element_type=F32
    ).astype(BF16)
    mixed = (wide_window + jnp.dot(context, w_out, preferred_element_type=F32)).astype(BF16)
    wide_mixed = mixed.astype(F32)
    act_one = jax.nn.silu(wide_mixed * norm_factor(wide_mixed) * gain_one)
    act_one = jnp.where(inside & (slot < 12), act_one, 0.0).astype(BF16)

    def own_columns(value):
        return value.reshape(ROWS, SLOTS, C)[:, 2:10].reshape(TILE, C)

    own_queries = own_columns(queries)
    own_scores = jnp.einsum("kd,qd->kq", keys, own_queries, preferred_element_type=F32)
    own_prob = jax.nn.softmax(own_scores * inverse_root, axis=0)
    query_key = lax.dot_general(own_queries, w_key, NT, preferred_element_type=F32).astype(BF16)

    def framed(f0, f1, f2):
        stacked = jnp.stack([f.reshape(ROWS, SLOTS, C) for f in (f0, f1, f2)])
        return jnp.pad(stacked, ((0, 0), (1, 1), (0, 0), (0, 0)))

    act_frames = framed(moved(act_one, 2), moved(act_one, 1), act_one)

    keep = lax.dynamic_index_in_dim(grad_out, row, 0, keepdims=False)
    give = lax.dynamic_index_in_dim(grad_out, 1 - row, 0, keepdims=False)
    got = lax.ppermute(give, "row", swap_row)
    tile = jnp.concatenate([jnp.where(row == 0, keep, got), jnp.where(row == 0, got, keep)], axis=0)
    to_right = [(i, i + 1) for i in range(cols - 1)]
    to_left = [(i + 1, i) for i in range(cols - 1)]
    grad = jnp.concatenate(
        [
            lax.ppermute(tile[:, 6:], "col", to_right),
            tile,
            lax.ppermute(tile[:, :2], "col", to_left),
            jnp.zeros((ROWS, 4, C), BF16),
        ],
        axis=1,
    ).reshape(SPAN, C)
    grad_frames = framed(grad, moved(grad, -1), moved(grad, -2))

    ours = jnp.where(core == 0, act_frames, grad_frames)
    theirs = lax.ppermute(jnp.where(core == 0, grad_frames, act_frames), "tm", swap_core)
    both = jnp.stack([ours, theirs], axis=2).reshape(3, (ROWS + 2) * 2 * SLOTS, C)
    both, mine, own_prob, query_key = lax.optimization_barrier((both, mine, own_prob, query_key))
    other = lax.ppermute(mine, "tm", swap_core)
    sums = pair_conv(core_arg, both, mine).reshape(ROWS, 2, SLOTS, C)
    kept = sums[:, 0].reshape(SPAN, C)
    given = lax.ppermute(sums[:, 1].reshape(SPAN, C).astype(BF16), "tm", swap_core)
    conv_one = jnp.where(core == 0, kept.astype(BF16), given)
    g_act_two = jnp.where(core == 0, given.astype(F32), kept)
    wide_conv = conv_one.astype(F32)
    pre_two = wide_conv * norm_factor(wide_conv) * gain_two
    g_conv = norm_backward(wide_conv, gain_two, g_act_two * silu_slope(pre_two))
    g_conv = jnp.where(inside, g_conv, 0.0).astype(BF16)
    g_conv = g_conv.reshape(ROWS, SLOTS, C)[:, 1:11].reshape(ROWS * 10, C)
    later = [moved(g_conv, -2), moved(g_conv, -1)]
    own_part = back_own(core_arg, g_conv, mine, other)
    g_mixed, partial = back_rest(
        core_arg,
        col_arg,
        later,
        (mine, other),
        (own_part, own_columns(grad), own_columns(mixed), gain_one.reshape(1, C)),
        (query_key, w_out, w_value, w_query),
        (own_prob, keys, values),
    )

    halves = g_mixed.reshape(2, 8, 8, C)
    stay = lax.dynamic_index_in_dim(halves, row, 0, keepdims=False)
    leave = lax.dynamic_index_in_dim(halves, 1 - row, 0, keepdims=False)
    come = lax.ppermute(leave, "row", swap_row)
    g_tile = jnp.stack([jnp.where(row == 0, stay, come), jnp.where(row == 0, come, stay)])
    parts = lax.all_to_all(partial.reshape(-1, 64, C), ("row", "col"), 0, 0, tiled=True)
    g_normed = jnp.sum(parts.reshape(2, cols, 64, C).astype(F32), axis=1).reshape(latent.shape)

    wide_latent = latent.astype(F32)
    return g_tile.astype(F32) + norm_backward(wide_latent, norm_gain, g_normed)


def solution(mesh):
    placed = (
        P("tm", "row", "col", None),
        P("tm", "row", "col", None),
        P(),
        P(),
        P(),
        P(),
        P(),
        P(),
        P(),
        P(None, None, None, "col", None),
        P(None, None, None, "col", None),
    )
    return jax.shard_map(
        shards, mesh=mesh, in_specs=placed, out_specs=P("tm", "row", "col", None), check_vma=False
    )
```
